32 devices in a mesh: variant: 4 (over y, x), sub: 8 (over z, core).
Axes of the slice: x: 2, y: 2, z: 4, core: 2. Of those that a mesh axis runs over, the one named last changes fastest.
Arguments:
- displacement: float32 [4, 6, 1024], P('variant', None, 'sub'), may hold values from -6 to 6
- neighbours: int32 [2, 1024], P(None, 'sub'), may hold values from 0 to 129, as said below
- micro_state: bfloat16 [4, 24576, 512], P('variant', 'sub'), may hold values from -6 to 6
- strain_loads: float32 [4, 6, 512], P('variant'), may hold values from -3 to 3
- stiffness: bfloat16 [4, 512, 512], P('variant'), may hold values from -0.25 to 0.25
- expand_weight: bfloat16 [4, 512, 2048], P('variant'), may hold values from -0.25 to 0.25
- contract_weight: bfloat16 [4, 2048, 512], P('variant'), may hold values from -0.125 to 0.125
- batch_route: int32 [4, 2, 192], P('variant', None, 'sub'), may hold values from -1 to 7, as said below
- yield_flags: int32 [4, 24576], P('variant', 'sub'), may hold values 0 or 1
- readout: bfloat16 [4, 512], P('variant'), may hold values from -0.75 to 0.75
- external_force: float32 [4, 1024], P('variant', 'sub'), may hold values from -6 to 6
- coarse_inverse: bfloat16 [4, 1024, 1024], P('variant', 'sub'), may hold values from -0.1875 to 0.1875
Outputs:
- states_next: bfloat16 [4, 24576, 512], P('variant', 'sub')
- coarse_correction: float32 [4, 1024], P('variant', 'sub')
The draws below stay inside these ranges and needn't reach their ends.
Inputs may be any that keep to these rules, and one draw needn't show every extreme that they name: `neighbours`: entry 0 is position i or i + 1 of macro point i within its device (i counted from 0 in the device), entry 1 is i + 1 or i + 2, and entry 1 exceeds entry 0; the first and last point of each device use i and i + 2. `batch_route`: entry 0 of a batch held by device s on sub is -1 or (s + d) % 8 for some d from 1 to 4, each d used by at most one batch of s; entry 1 is -1 where entry 0 is, else its slot there, 0 to 1. Batches sent to one device have different slots; every device receives at most 2 batches, and in every draw some device receives 2.
All inputs are finite; a program needn't handle non-finite values. No bound on the sum of `yield_flags` on one device may be relied on, other than what follows from the above.
Results may differ from the reference program's by a relative error of at most 0.0055.
Values may be sent and summed in bfloat16 or wider, within the bound.
No kernel may reach another device: no remote copies, remote signals or barrier semaphores. Data moves between devices by JAX's collectives and lax.ppermute only.
A program may use at most 64 MiB of HBM per device.

```python
import jax
import jax.numpy as jnp
from jax import lax

MP_DEV = 128
RPP = 24
BATCH = 128
MODES = 512
HIDDEN_SIZE = 2048
STRAIN = 6
VARIANTS = 4
COARSE = 1024
ROWS = 24576
BAT_DEV = 24
SPREAD = 4
CAP = 2
N_SUB = 8


def draw_neighbours(key, part):
    key = jax.random.fold_in(key, 17)
    total = MP_DEV * N_SUB
    pattern = jax.random.randint(key, (total,), 0, 3)
    position = jnp.arange(total) % MP_DEV
    pattern = jnp.where((position == 0) | (position == MP_DEV - 1), 0, pattern)
    centre = position + 1
    lower_index = jnp.where(pattern == 2, centre, centre - 1)
    upper_index = jnp.where(pattern == 1, centre, centre + 1)
    return jnp.stack([lower_index, upper_index]).astype(jnp.int32)


def draw_batch_route(key, part):
    key = jax.random.fold_in(key, 29)

    def per_variant(variant_key):
        key_phase, key_full, key_shift, key_order, key_chance = jax.random.split(variant_key, 5)
        phase = jax.random.randint(key_phase, (), 0, SPREAD)
        full_target = jax.random.randint(key_full, (), 0, N_SUB)
        batch_shift = jax.random.randint(key_shift, (N_SUB,), 0, BAT_DEV)
        order = jax.random.permutation(key_order, BAT_DEV)[:SPREAD]
        chance = jax.random.randint(key_chance, (N_SUB, SPREAD), 0, 4)
        sender = jnp.arange(N_SUB)[:, None]
        step_ahead = jnp.arange(1, SPREAD + 1)[None, :]
        receiver = (sender + step_ahead) % N_SUB
        rank = (sender + phase) % SPREAD
        is_hot = rank < CAP
        alive = is_hot & ((chance < 3) | (receiver == full_target))
        batch_index = sender * BAT_DEV + (batch_shift[:, None] + order[None, :]) % BAT_DEV
        landing = jnp.where(alive, batch_index, N_SUB * BAT_DEV).reshape(-1)
        target_list = jnp.full((N_SUB * BAT_DEV,), -1, jnp.int32).at[landing].set(receiver.reshape(-1).astype(jnp.int32), mode='drop')
        slot_list = jnp.full((N_SUB * BAT_DEV,), -1, jnp.int32).at[landing].set(jnp.broadcast_to(rank, (N_SUB, SPREAD)).reshape(-1).astype(jnp.int32), mode='drop')
        return jnp.stack([target_list, slot_list])
    variant_keys = jax.random.split(key, VARIANTS)
    return jax.vmap(per_variant)(variant_keys).astype(jnp.int32)


def set_ends(values, own_key, least, top_value):
    longest = values.shape.index(max(values.shape))
    spots = []
    for shift in (0, 1):
        where = [jax.random.randint(jax.random.fold_in(own_key, axis), (), 0, length) for axis, length in enumerate(values.shape)]
        where[longest] = (where[longest] + shift) % values.shape[longest]
        spots.append(tuple(where))
    return values.at[spots[0]].set(least).at[spots[1]].set(top_value)


def block_levels(stream_key, shape, shards, least, high):
    level, own = 1.0, jax.random.fold_in(stream_key, 6)
    for dim, blocks in shards:
        draws = jnp.exp(jax.random.uniform(jax.random.fold_in(own, dim), (blocks,), jnp.float32, least / len(shards), high / len(shards)))
        level = level * jnp.repeat(draws, shape[dim] // blocks).reshape([-1 if axis == dim else 1 for axis in range(len(shape))])
    return level


def bell_draw(own_key, extent, width, most, cuts=(), held_as=jnp.bfloat16):
    loudness = block_levels(own_key, extent, cuts, -0.22, 0.18) if cuts else 1.0
    result = jax.random.normal(own_key, extent, jnp.float32) * width * loudness
    return jnp.minimum(jnp.maximum(result, -most), most).astype(held_as)


def setup_inputs(seed: int = 0) -> dict:
    splits = jax.random.split(jax.random.key(seed), 13)
    displacement = bell_draw(splits[0], (VARIANTS, STRAIN, COARSE), 1.0, 6.0, ((0, 4), (2, 8)), jnp.float32)
    neighbours = draw_neighbours(jax.random.fold_in(splits[12], 71), 0)
    micro_state = bell_draw(splits[2], (VARIANTS, ROWS, MODES), 1.0, 6.0, ((0, 4), (1, 8)))
    strain_loads = bell_draw(splits[3], (VARIANTS, STRAIN, MODES), 4 ** -0.5, 3.0, ((0, 4),), jnp.float32)
    stiffness = bell_draw(splits[4], (VARIANTS, MODES, MODES), MODES ** -0.5, 0.25, ((0, 4),))
    expand_weight = bell_draw(splits[5], (VARIANTS, MODES, HIDDEN_SIZE), MODES ** -0.5, 0.25, ((0, 4),))
    contract_weight = bell_draw(splits[6], (VARIANTS, HIDDEN_SIZE, MODES), HIDDEN_SIZE ** -0.5, 0.125, ((0, 4),))
    batch_route = draw_batch_route(jax.random.fold_in(splits[12], 71), 0)
    yield_flags = set_ends((jax.random.randint(splits[8], (VARIANTS, ROWS), 0, 2) < 1).astype(jnp.int32), jax.random.fold_in(splits[8], 1), 0, 1)
    readout = bell_draw(splits[9], (VARIANTS, MODES), (MODES // 8) ** -0.5, 0.75, ((0, 4),))
    external_force = bell_draw(splits[10], (VARIANTS, COARSE), 1.0, 6.0, ((0, 4), (1, 8)), jnp.float32)
    coarse_inverse = bell_draw(splits[11], (VARIANTS, COARSE, COARSE), COARSE ** -0.5, 0.1875, ((0, 4), (1, 8)))
    return {"displacement": displacement, "neighbours": neighbours, "micro_state": micro_state, "strain_loads": strain_loads, "stiffness": stiffness, "expand_weight": expand_weight, "contract_weight": contract_weight, "batch_route": batch_route, "yield_flags": yield_flags, "readout": readout, "external_force": external_force, "coarse_inverse": coarse_inverse}


def plastic_update(row_block, expand_weight, contract_weight):
    hidden = jax.nn.silu(jnp.dot(row_block, expand_weight, preferred_element_type=jnp.float32)).astype(jnp.bfloat16)
    return jnp.dot(hidden, contract_weight, preferred_element_type=jnp.float32).astype(jnp.bfloat16)


def reference(displacement, neighbours, micro_state, strain_loads, stiffness, expand_weight, contract_weight, batch_route, yield_flags, readout, external_force, coarse_inverse):
    points = displacement.shape[2]
    owner_base = (jnp.arange(points) // MP_DEV).astype(jnp.int32) * MP_DEV
    first_index = owner_base + neighbours[0].astype(jnp.int32)
    second_index = owner_base + neighbours[1].astype(jnp.int32)
    spacing = (neighbours[1] - neighbours[0]).astype(jnp.float32)
    batch_count = ROWS // BATCH
    slot_total = N_SUB * SPREAD
    sender = (jnp.arange(batch_count) // BAT_DEV).astype(jnp.int32)

    def variant_step(inputs):
        macro_field, state_rows, load_rows, stiff_matrix, w_up, w_down, route_rows, flag_rows, readout_vec, force_rows, inverse = inputs
        padded = jnp.pad(macro_field, ((0, 0), (1, 1)))
        strain = (padded[:, second_index] - padded[:, first_index]) / spacing
        per_row = jnp.repeat(strain, RPP, axis=1)
        trial_state = state_rows.astype(jnp.float32) + jnp.dot(per_row.T, load_rows, precision=lax.Precision.HIGHEST)
        elastic = jnp.dot(trial_state.astype(jnp.bfloat16), stiff_matrix, preferred_element_type=jnp.float32)
        elastic_half = elastic.astype(jnp.bfloat16)
        batches = elastic_half.reshape(batch_count, BATCH, MODES)
        target = route_rows[0].astype(jnp.int32)
        alive_batch = target >= 0
        offset = (target - sender) % N_SUB
        position = jnp.where(alive_batch, sender * SPREAD + offset - 1, slot_total).astype(jnp.int32)
        slot_table = jnp.full((slot_total,), batch_count, jnp.int32).at[position].set(jnp.arange(batch_count, dtype=jnp.int32), mode="drop")
        with_blank = jnp.concatenate([batches, jnp.zeros((1, BATCH, MODES), jnp.bfloat16)], axis=0)
        received = with_blank[slot_table]
        updated = lax.map(lambda block_rows: plastic_update(block_rows, w_up, w_down), received)
        handed_back = updated[jnp.minimum(position, slot_total - 1)]
        handed_back = jnp.where(alive_batch[:, None, None], handed_back, jnp.zeros_like(handed_back))
        correction = handed_back.reshape(ROWS, MODES).astype(jnp.float32)
        weight_rows = (jnp.repeat(alive_batch.astype(jnp.int32), BATCH) * flag_rows).astype(jnp.float32)
        next_state = (elastic + weight_rows[:, None] * correction).astype(jnp.bfloat16)
        projected = jnp.dot(next_state, readout_vec, preferred_element_type=jnp.float32)
        averaged = jnp.mean(projected.reshape(points, RPP), axis=1)
        residual = (force_rows - averaged).astype(jnp.bfloat16)
        coarse = jnp.dot(inverse, residual, preferred_element_type=jnp.float32)
        return next_state, coarse

    return lax.map(variant_step, (displacement, micro_state, strain_loads, stiffness, expand_weight, contract_weight, batch_route, yield_flags, readout, external_force, coarse_inverse))
```

```python
import functools

import jax
import jax.numpy as jnp
from jax import lax
from jax.experimental import pallas as pl
from jax.experimental.pallas import tpu as pltpu
from jax.sharding import PartitionSpec as P

BATCH = 128
GROUP = 8
TILE = 32
MIB = 1 << 20
F32 = jnp.float32
BF16 = jnp.bfloat16
NT = (((1,), (1,)), ((), ()))


def dot(a, b):
    return jnp.dot(a, b, preferred_element_type=F32)


def dot_nt(a, b, precision=None):
    return lax.dot_general(a, b, NT, precision=precision, preferred_element_type=F32)


def halves(x):
    high = x.astype(BF16)
    return high, (x - high.astype(F32)).astype(BF16)


def silu(a):
    half = 0.5 * a
    return half + half * jnp.tanh(half)


def list_alive(route_ref, list_ref, batches):
    count = jnp.int32(0)
    for b in range(batches):
        list_ref[count] = jnp.int32(b)
        count = count + (route_ref[0, 0, b] >= 0).astype(jnp.int32)
    return count


def step_kernel(
    per_point,
    width,
    core_ref,
    chip_ref,
    pick_ref,
    *refs,
):
    sources, outs, rest = refs[:11], refs[11:13], refs[13:]
    held_refs = sources
    route_ref, displacement_ref, neighbours_ref, loads_ref, readout_ref, force_ref, flags_ref = held_refs[:7]
    state_ref, stiffness_ref, expand_ref, contract_ref = held_refs[7:]
    out_ref, residual_ref = outs
    list_ref, next_ref, hidden_ref, point_ref, sum_ref, out_sems, batch_sems = rest
    points = displacement_ref.shape[2]
    rows, modes = state_ref.shape[1:]
    batches = rows // BATCH
    tile_points = TILE
    tile = tile_points * per_point
    tiles = points // tile_points
    spans = [slice(t * tile, (t + 1) * tile) for t in range(tiles)]

    count = list_alive(route_ref, list_ref, batches)

    odd = lax.axis_index("sub") % 2 == 1
    own, core, chip = (
        jnp.concatenate([ref[k] for k in range(ref.shape[0])], axis=0)
        for ref in (displacement_ref, core_ref, chip_ref)
    )
    before = jnp.where(odd, core, chip)
    after = jnp.where(odd, chip, core)
    place = lax.broadcasted_iota(jnp.int32, own.shape, 1)
    left = jnp.where(place == 0, pltpu.roll(before, 1, 1), pltpu.roll(own, 1, 1))
    right = jnp.where(
        place == points - 1, pltpu.roll(after, points - 1, 1), pltpu.roll(own, points - 1, 1)
    )
    first, second = neighbours_ref[0:1, :], neighbours_ref[1:2, :]
    lower = jnp.where(first == place, left, own)
    upper = jnp.where(second == place + 2, right, own)
    strain = (upper - lower) / (second - first).astype(F32)
    loads = jnp.concatenate([loads_ref[k] for k in range(loads_ref.shape[0])], axis=0)
    load = lax.dot_general(
        strain,
        loads,
        (((0,), (0,)), ((), ())),
        precision=lax.Precision.HIGHEST,
        preferred_element_type=F32,
    )
    stiffness = stiffness_ref[0]
    shift = dot(jnp.concatenate(halves(load), axis=0), stiffness)
    point_ref[...] = shift[:points, :] + shift[points:, :]

    outgoing = [
        pltpu.make_async_copy(next_ref.at[s, :], out_ref.at[0, s, :], out_sems.at[t])
        for t, s in enumerate(spans)
    ]
    for t, span in enumerate(spans):
        acc = dot(state_ref[0, span, :], stiffness)
        shift = point_ref[t * tile_points : (t + 1) * tile_points, :]
        acc = acc.reshape(tile_points, per_point, modes) + shift[:, None, :]
        next_ref[span, :] = acc.reshape(tile, modes).astype(BF16)
        outgoing[t].start()
    for copy in outgoing:
        copy.wait()

    @pl.loop(0, (count + width - 1) // width)
    def _(c):
        chosen = [list_ref[jnp.minimum(c * width + j, count - 1)] for j in range(width)]
        starts = [pl.multiple_of(b * BATCH, BATCH) for b in chosen]
        taken = jnp.concatenate([next_ref[pl.ds(s, BATCH), :] for s in starts], axis=0)
        for h in range(0, expand_ref.shape[2], 512):
            hidden_ref[:, h : h + 512] = silu(dot(taken, expand_ref[0, :, h : h + 512])).astype(BF16)
        correction = dot(hidden_ref[...], contract_ref[0])
        for j, s in enumerate(starts):
            at = slice(j * BATCH, (j + 1) * BATCH)
            flags = flags_ref[0:1, pl.ds(s, BATCH)].astype(F32)
            column = jnp.broadcast_to(flags, (BATCH, BATCH)).T
            column = jnp.concatenate([column] * (modes // BATCH), axis=1)
            next_ref[pl.ds(s, BATCH), :] = (taken[at, :].astype(F32) + column * correction[at, :]).astype(BF16)

    def changed(i):
        s = pl.multiple_of(list_ref[i] * BATCH, BATCH)
        span = pl.ds(s, BATCH)
        return pltpu.make_async_copy(next_ref.at[span, :], out_ref.at[0, span, :], batch_sems)

    @pl.loop(0, count)
    def _(i):
        changed(i).start()

    for t, span in enumerate(spans):
        sum_ref[t * tile_points : (t + 1) * tile_points, :] = dot(pick_ref[...], next_ref[span, :])
    readout = jnp.broadcast_to(readout_ref[...], (GROUP, modes)).astype(F32)
    mean = dot_nt(readout, sum_ref[...], lax.Precision.HIGHEST)[0:1, :] * (1.0 / per_point)
    residual_ref[...] = (force_ref[...] - mean).astype(BF16)

    @pl.loop(0, count)
    def _(i):
        changed(i).wait()


def pick_kernel(per_point, pick_ref):
    shape = pick_ref.shape
    p = lax.broadcasted_iota(jnp.int32, shape, 0)
    r = lax.broadcasted_iota(jnp.int32, shape, 1)
    pick_ref[...] = jnp.where((r >= p * per_point) & (r < (p + 1) * per_point), 1.0, 0.0).astype(BF16)


def coarse_kernel(inverse_ref, *refs):
    pairs, out_ref = refs[:-1], refs[-1]
    points = out_ref.shape[1]
    me = lax.axis_index("sub")
    total = jnp.zeros((GROUP, points), F32)
    for k, pair_ref in enumerate(pairs):
        chip = (me // 2) ^ k
        for c in range(2):
            block = pl.multiple_of((2 * chip + (me + c) % 2) * points, points)
            part = jnp.broadcast_to(pair_ref[c : c + 1, :], (GROUP, points))
            total = total + dot_nt(part, inverse_ref[0, :, pl.ds(block, points)])
    out_ref[...] = total[0:1, :]


def swap_pairs(n, offset):
    pairs = [(i, i + 1) for i in range(offset, n - 1, 2)]
    return pairs + [(j, i) for i, j in pairs]


def on_device(
    displacement,
    neighbours,
    micro_state,
    strain_loads,
    stiffness,
    expand_weight,
    contract_weight,
    batch_route,
    yield_flags,
    readout,
    external_force,
    coarse_inverse,
):
    n = lax.axis_size("sub")
    points = displacement.shape[2]
    rows, modes = micro_state.shape[1:]
    hidden_size = expand_weight.shape[2]
    per_point = rows // points
    batches = rows // BATCH
    width = min(4, n // 2, batches)
    field = jnp.transpose(displacement, (1, 0, 2))
    vmem = pl.BlockSpec(memory_space=pltpu.VMEM)
    pick = pl.pallas_call(
        functools.partial(pick_kernel, per_point),
        out_shape=jax.ShapeDtypeStruct((TILE, TILE * per_point), BF16),
        out_specs=vmem,
        compiler_params=pltpu.CompilerParams(vmem_limit_bytes=MIB),
        cost_estimate=pl.CostEstimate(flops=20 * 10**9, bytes_accessed=MIB, transcendentals=0),
    )()
    loads = jnp.transpose(strain_loads, (1, 0, 2))
    from_core = lax.ppermute(field, "sub", swap_pairs(n, 0))
    from_chip = lax.ppermute(field, "sub", swap_pairs(n, 1))
    hbm = pl.BlockSpec(memory_space=pltpu.HBM)
    sources = (
        batch_route,
        field,
        neighbours,
        loads,
        readout,
        external_force,
        yield_flags,
        micro_state,
        stiffness,
        expand_weight,
        contract_weight,
    )
    tiles = points // TILE
    states_next, residual = pl.pallas_call(
        functools.partial(step_kernel, per_point, width),
        out_shape=(
            jax.ShapeDtypeStruct((1, rows, modes), BF16),
            jax.ShapeDtypeStruct((1, points), BF16),
        ),
        in_specs=[vmem] * 3 + [pl.BlockSpec(memory_space=pltpu.SMEM)] + [vmem] * (len(sources)-1),
        out_specs=(hbm, vmem),
        scratch_shapes=[
            pltpu.SMEM((batches + 1,), jnp.int32),
            pltpu.VMEM((rows, modes), BF16),
            pltpu.VMEM((width * BATCH, hidden_size), BF16),
            pltpu.VMEM((points, modes), F32),
            pltpu.VMEM((points, modes), F32),
            pltpu.SemaphoreType.DMA((tiles,)),
            pltpu.SemaphoreType.DMA(()),
        ],
        compiler_params=pltpu.CompilerParams(vmem_limit_bytes=24 * MIB),
        cost_estimate=pl.CostEstimate(
            flops=2 * rows * modes * modes + 4 * width * BATCH * modes * hidden_size,
            bytes_accessed=11 * MIB,
            transcendentals=0,
        ),
    )(from_core, from_chip, pick, *sources)
    other = lax.ppermute(residual, "sub", swap_pairs(n, 0))
    pair = jnp.concatenate([residual, other], axis=0)
    pairs = [pair] + [
        lax.ppermute(pair, "sub", [(i, i ^ (2 * k)) for i in range(n)]) for k in range(1, n // 2)
    ]
    coarse = pl.pallas_call(
        coarse_kernel,
        out_shape=jax.ShapeDtypeStruct((1, points), F32),
        in_specs=[vmem] * (1 + len(pairs)),
        out_specs=vmem,
        compiler_params=pltpu.CompilerParams(vmem_limit_bytes=4 * MIB),
    )(coarse_inverse, *pairs)
    return (states_next, coarse)


def solution(mesh):
    return jax.shard_map(
        on_device,
        mesh=mesh,
        in_specs=(
            P("variant", None, "sub"),
            P(None, "sub"),
            P("variant", "sub", None),
            P("variant", None, None),
            P("variant", None, None),
            P("variant", None, None),
            P("variant", None, None),
            P("variant", None, "sub"),
            P("variant", "sub"),
            P("variant", None),
            P("variant", "sub"),
            P("variant", "sub", None),
        ),
        out_specs=(P("variant", "sub", None), P("variant", "sub")),
        check_vma=False,
    )
```

```python
import functools

import jax
import jax.numpy as jnp
from jax import lax
from jax.experimental import pallas as pl
from jax.experimental.pallas import tpu as pltpu
from jax.sharding import PartitionSpec as P

BATCH = 128
GROUP = 8
TILE = 32
EDGE = 2
NEAR_CHIPS = 4
MIB = 1 << 20
F32 = jnp.float32
BF16 = jnp.bfloat16
NT = (((1,), (1,)), ((), ()))


def dot(a, b):
    return jnp.dot(a, b, preferred_element_type=F32)


def dot_nt(a, b, precision=None):
    return lax.dot_general(a, b, NT, precision=precision, preferred_element_type=F32)


def halves(x):
    high = x.astype(BF16)
    return high, (x - high.astype(F32)).astype(BF16)


def silu(a):
    half = 0.5 * a
    return half + half * jnp.tanh(half)


def list_alive(route_ref, list_ref, batches):
    count = jnp.int32(0)
    for b in range(batches):
        list_ref[count] = jnp.int32(b)
        count = count + (route_ref[0, 0, b] >= 0).astype(jnp.int32)
    return count


def stack_rows(ref):
    return jnp.concatenate([ref[k] for k in range(ref.shape[0])], axis=0)


def strain_of(own, before, after, neighbours_ref):
    points = own.shape[1]
    place = lax.broadcasted_iota(jnp.int32, own.shape, 1)
    left = jnp.where(place == 0, before, pltpu.roll(own, 1, 1))
    right = jnp.where(place == points - 1, after, pltpu.roll(own, points - 1, 1))
    first, second = neighbours_ref[0:1, :], neighbours_ref[1:2, :]
    lower = jnp.where(first == place, left, own)
    upper = jnp.where(second == place + 2, right, own)
    return (upper - lower) / (second - first).astype(F32)


def elastic_kernel(
    per_point,
    pick_ref,
    field_ref,
    neighbours_ref,
    loads_ref,
    stiffness_ref,
    state_ref,
    elastic_ref,
    sum_ref,
    point_ref,
):
    own = stack_rows(field_ref)
    points = own.shape[1]
    modes = state_ref.shape[2]
    tile = TILE * per_point
    strain = strain_of(own, jnp.zeros_like(own), jnp.zeros_like(own), neighbours_ref)
    load = lax.dot_general(
        strain,
        stack_rows(loads_ref),
        (((0,), (0,)), ((), ())),
        precision=lax.Precision.HIGHEST,
        preferred_element_type=F32,
    )
    stiffness = stiffness_ref[0]
    shift = dot(jnp.concatenate(halves(load), axis=0), stiffness)
    point_ref[...] = shift[:points, :] + shift[points:, :]
    for t in range(points // TILE):
        span, at = slice(t * tile, (t + 1) * tile), slice(t * TILE, (t + 1) * TILE)
        acc = dot(state_ref[0, span, :], stiffness)
        acc = acc.reshape(TILE, per_point, modes) + point_ref[at, :][:, None, :]
        elastic_ref[span, :] = acc.reshape(tile, modes).astype(BF16)
        sum_ref[at, :] = dot(pick_ref[...], elastic_ref[span, :])


def plastic_kernel(
    per_point,
    width,
    route_ref,
    core_ref,
    chip_ref,
    field_ref,
    neighbours_ref,
    loads_ref,
    stiffness_ref,
    state_ref,
    expand_ref,
    contract_ref,
    flags_ref,
    readout_ref,
    force_ref,
    elastic_ref,
    start_ref,
    out_ref,
    residual_ref,
    list_ref,
    sum_ref,
    edge_ref,
    taken_ref,
    hidden_ref,
    next_ref,
    bulk_sem,
    edge_sems,
    batch_sem,
):
    rows, modes = elastic_ref.shape
    points = rows // per_point
    batches = rows // BATCH
    edge = EDGE * per_point
    middle = slice(edge, rows - edge)
    bulk = pltpu.make_async_copy(elastic_ref.at[middle, :], out_ref.at[0, middle, :], bulk_sem)
    bulk.start()

    odd = lax.axis_index("sub") % 2 == 1
    own, core, chip = stack_rows(field_ref), stack_rows(core_ref), stack_rows(chip_ref)
    before = pltpu.roll(jnp.where(odd, core, chip), 1, 1)
    after = pltpu.roll(jnp.where(odd, chip, core), points - 1, 1)
    strain = strain_of(own, before, after, neighbours_ref)
    loads = stack_rows(loads_ref)
    near = [p % points for p in range(-EDGE, EDGE)]
    near = near[EDGE:] + near[:EDGE]
    load = jnp.concatenate(
        [jnp.sum(strain[:, p : p + 1] * loads, axis=0, keepdims=True) for p in near], axis=0
    )
    high, low = halves(load)
    blank = jnp.zeros((GROUP, modes), F32)
    extra = jnp.concatenate([high.astype(F32), low.astype(F32), blank], axis=0).astype(BF16)
    ends = [slice(0, edge), slice(rows - edge, rows)]
    acc = dot(
        jnp.concatenate([state_ref[0, s, :] for s in ends] + [extra], axis=0), stiffness_ref[0]
    )
    shift = acc[2 * edge : 2 * edge + 2 * EDGE, :] + acc[2 * edge + 2 * EDGE : 2 * edge + 4 * EDGE, :]
    fixed = acc[: 2 * edge, :].reshape(2 * EDGE, per_point, modes) + shift[:, None, :]
    fixed = fixed.reshape(2 * edge, modes).astype(BF16)
    edge_ref[...] = fixed
    totals = jnp.sum(fixed.astype(F32).reshape(2 * EDGE, per_point, modes), axis=1)
    sum_ref[...] = start_ref[...]
    sum_ref[0:EDGE, :] = totals[:EDGE, :]
    sum_ref[points - EDGE : points, :] = totals[EDGE:, :]
    edges = [
        pltpu.make_async_copy(edge_ref.at[i * edge : (i + 1) * edge, :], out_ref.at[0, s, :], edge_sems.at[i])
        for i, s in enumerate(ends)
    ]
    for copy in edges:
        copy.start()

    count = list_alive(route_ref, list_ref, batches)

    @pl.loop(0, (count + width - 1) // width)
    def _(c):
        chosen = [list_ref[jnp.minimum(c * width + j, count - 1)] for j in range(width)]
        starts = [pl.multiple_of(b * BATCH, BATCH) for b in chosen]
        for j, (b, s) in enumerate(zip(chosen, starts)):
            taken_ref[j * BATCH : (j + 1) * BATCH, :] = elastic_ref[pl.ds(s, BATCH), :]

            @pl.when(b == 0)
            def _():
                taken_ref[j * BATCH : j * BATCH + edge, :] = edge_ref[:edge, :]

            @pl.when(b == batches - 1)
            def _():
                taken_ref[(j + 1) * BATCH - edge : (j + 1) * BATCH, :] = edge_ref[edge:, :]

        taken = taken_ref[...]
        for h in range(0, expand_ref.shape[2], 512):
            hidden_ref[:, h : h + 512] = silu(dot(taken, expand_ref[0, :, h : h + 512])).astype(BF16)
        correction = dot(hidden_ref[...], contract_ref[0])
        p = lax.broadcasted_iota(jnp.int32, (points, BATCH), 0) * per_point
        r = lax.broadcasted_iota(jnp.int32, (points, BATCH), 1)
        owners, changes = [], []
        for j, s in enumerate(starts):
            at = slice(j * BATCH, (j + 1) * BATCH)
            flags = flags_ref[0:1, pl.ds(s, BATCH)].astype(F32)
            column = jnp.broadcast_to(flags, (BATCH, BATCH)).T
            column = jnp.concatenate([column] * (modes // BATCH), axis=1)
            change = column * correction[at, :]
            slot = pl.multiple_of((c * width + j) * BATCH, BATCH)
            next_ref[pl.ds(slot, BATCH), :] = (taken[at, :].astype(F32) + change).astype(BF16)
            row = r + jnp.where(c * width + j < count, s, -rows)
            owners.append(jnp.where((row >= p) & (row < p + per_point), 1.0, 0.0).astype(BF16))
            changes.append(change.astype(BF16))
        sum_ref[...] += dot(jnp.concatenate(owners, axis=1), jnp.concatenate(changes, axis=0))

    for copy in [bulk] + edges:
        copy.wait()

    def changed(i):
        source = pl.ds(pl.multiple_of(i * BATCH, BATCH), BATCH)
        target = pl.ds(pl.multiple_of(list_ref[i] * BATCH, BATCH), BATCH)
        return pltpu.make_async_copy(next_ref.at[source, :], out_ref.at[0, target, :], batch_sem)

    @pl.loop(0, count)
    def _(i):
        changed(i).start()

    readout = jnp.broadcast_to(readout_ref[...], (GROUP, modes)).astype(F32)
    mean = dot_nt(readout, sum_ref[...], lax.Precision.HIGHEST)[0:1, :] * (1.0 / per_point)
    residual_ref[...] = (force_ref[...] - mean).astype(BF16)

    @pl.loop(0, count)
    def _(i):
        changed(i).wait()


def pick_kernel(per_point, pick_ref):
    shape = pick_ref.shape
    p = lax.broadcasted_iota(jnp.int32, shape, 0)
    r = lax.broadcasted_iota(jnp.int32, shape, 1)
    pick_ref[...] = jnp.where((r >= p * per_point) & (r < (p + 1) * per_point), 1.0, 0.0).astype(BF16)


def coarse_kernel(inverse_ref, *refs):
    pairs, out_ref = refs[:-1], refs[-1]
    points = out_ref.shape[1]
    me = lax.axis_index("sub")
    total = jnp.zeros((GROUP, points), F32)
    for k, pair_ref in enumerate(pairs):
        chip = (me // 2) ^ k
        for c in range(2):
            block = pl.multiple_of((2 * chip + (me + c) % 2) * points, points)
            part = jnp.broadcast_to(pair_ref[c : c + 1, :], (GROUP, points))
            total = total + dot_nt(part, inverse_ref[0, :, pl.ds(block, points)])
    out_ref[...] = total[0:1, :]


def swap_pairs(n, offset):
    pairs = [(i, i + 1) for i in range(offset, n - 1, 2)]
    return pairs + [(j, i) for i, j in pairs]


def on_device(
    displacement,
    neighbours,
    micro_state,
    strain_loads,
    stiffness,
    expand_weight,
    contract_weight,
    batch_route,
    yield_flags,
    readout,
    external_force,
    coarse_inverse,
):
    n = lax.axis_size("sub")
    points = displacement.shape[2]
    rows, modes = micro_state.shape[1:]
    hidden_size = expand_weight.shape[2]
    per_point = rows // points
    batches = rows // BATCH
    reach = min(16, n // 2, batches)
    width = min(4, reach)
    slots = -(-reach // width) * width
    field = jnp.transpose(displacement, (1, 0, 2))
    loads = jnp.transpose(strain_loads, (1, 0, 2))
    vmem = pl.BlockSpec(memory_space=pltpu.VMEM)
    pick = pl.pallas_call(
        functools.partial(pick_kernel, per_point),
        out_shape=jax.ShapeDtypeStruct((TILE, TILE * per_point), BF16),
        out_specs=vmem,
        compiler_params=pltpu.CompilerParams(vmem_limit_bytes=MIB),
        cost_estimate=pl.CostEstimate(flops=20 * 10**9, bytes_accessed=MIB, transcendentals=0),
    )()
    from_core = lax.ppermute(field, "sub", swap_pairs(n, 0))
    from_chip = lax.ppermute(field, "sub", swap_pairs(n, 1))
    elastic, sums = pl.pallas_call(
        functools.partial(elastic_kernel, per_point),
        out_shape=(
            jax.ShapeDtypeStruct((rows, modes), BF16),
            jax.ShapeDtypeStruct((points, modes), F32),
        ),
        in_specs=[vmem] * 6,
        out_specs=(vmem, vmem),
        scratch_shapes=[pltpu.VMEM((points, modes), F32)],
        compiler_params=pltpu.CompilerParams(vmem_limit_bytes=20 * MIB),
        cost_estimate=pl.CostEstimate(
            flops=2 * rows * modes * modes, bytes_accessed=8 * MIB, transcendentals=0
        ),
    )(pick, field, neighbours, loads, stiffness, micro_state)
    states_next, residual = pl.pallas_call(
        functools.partial(plastic_kernel, per_point, width),
        out_shape=(
            jax.ShapeDtypeStruct((1, rows, modes), BF16),
            jax.ShapeDtypeStruct((1, points), BF16),
        ),
        in_specs=[pl.BlockSpec(memory_space=pltpu.SMEM)] + [vmem] * 14,
        out_specs=(pl.BlockSpec(memory_space=pltpu.HBM), vmem),
        scratch_shapes=[
            pltpu.SMEM((batches + 1,), jnp.int32),
            pltpu.VMEM((points, modes), F32),
            pltpu.VMEM((2 * EDGE * per_point, modes), BF16),
            pltpu.VMEM((width * BATCH, modes), BF16),
            pltpu.VMEM((width * BATCH, hidden_size), BF16),
            pltpu.VMEM((slots * BATCH, modes), BF16),
            pltpu.SemaphoreType.DMA(()),
            pltpu.SemaphoreType.DMA((2,)),
            pltpu.SemaphoreType.DMA(()),
        ],
        compiler_params=pltpu.CompilerParams(vmem_limit_bytes=28 * MIB),
        cost_estimate=pl.CostEstimate(
            flops=4 * width * BATCH * modes * hidden_size, bytes_accessed=8 * MIB, transcendentals=0
        ),
    )(
        batch_route,
        from_core,
        from_chip,
        field,
        neighbours,
        loads,
        stiffness,
        micro_state,
        expand_weight,
        contract_weight,
        yield_flags,
        readout,
        external_force,
        elastic,
        sums,
    )
    if n // 2 > NEAR_CHIPS:
        everyone = lax.all_gather(residual, "sub", axis=1, tiled=True)[0]
        return states_next, dot(coarse_inverse[0], everyone)[None]
    other = lax.ppermute(residual, "sub", swap_pairs(n, 0))
    pair = jnp.concatenate([residual, other], axis=0)
    pairs = [pair] + [
        lax.ppermute(pair, "sub", [(i, i ^ (2 * k)) for i in range(n)]) for k in range(1, n // 2)
    ]
    coarse = pl.pallas_call(
        coarse_kernel,
        out_shape=jax.ShapeDtypeStruct((1, points), F32),
        in_specs=[vmem] * (1 + len(pairs)),
        out_specs=vmem,
        compiler_params=pltpu.CompilerParams(vmem_limit_bytes=4 * MIB),
    )(coarse_inverse, *pairs)
    return (states_next, coarse)


def solution(mesh):
    return jax.shard_map(
        on_device,
        mesh=mesh,
        in_specs=(
            P("variant", None, "sub"),
            P(None, "sub"),
            P("variant", "sub", None),
            P("variant", None, None),
            P("variant", None, None),
            P("variant", None, None),
            P("variant", None, None),
            P("variant", None, "sub"),
            P("variant", "sub"),
            P("variant", None),
            P("variant", "sub"),
            P("variant", "sub", None),
        ),
        out_specs=(P("variant", "sub", None), P("variant", "sub")),
        check_vma=False,
    )
```

```python
import functools

import jax
import jax.numpy as jnp
from jax import lax
from jax.experimental import pallas as pl
from jax.experimental.pallas import tpu as pltpu
from jax.sharding import PartitionSpec as P

BATCH = 128
GROUP = 8
TILE = 32
EDGE = 2
NEAR_CHIPS = 4
MIB = 1 << 20
F32 = jnp.float32
BF16 = jnp.bfloat16
NT = (((1,), (1,)), ((), ()))


def dot(a, b):
    return jnp.dot(a, b, preferred_element_type=F32)


def dot_nt(a, b, precision=None):
    return lax.dot_general(a, b, NT, precision=precision, preferred_element_type=F32)


def halves(x):
    high = x.astype(BF16)
    return high, (x - high.astype(F32)).astype(BF16)


def silu(a):
    half = 0.5 * a
    return half + half * jnp.tanh(half)


def list_alive(route_ref, list_ref, batches):
    count = jnp.int32(0)
    for b in range(batches):
        list_ref[count] = jnp.int32(b)
        count = count + (route_ref[0, 0, b] >= 0).astype(jnp.int32)
    return count


def stack_rows(ref):
    return jnp.concatenate([ref[k] for k in range(ref.shape[0])], axis=0)


def thirds(x):
    high = x.astype(BF16).astype(F32)
    middle = (x - high).astype(BF16).astype(F32)
    return high, middle, x - high - middle


def spread(strain, loads):
    blank = [jnp.zeros((GROUP - strain.shape[0] % GROUP, x.shape[1]), F32) for x in (strain, loads)]
    a, b, c = (jnp.concatenate([x, blank[0]], axis=0) for x in thirds(strain))
    d, e, f = (jnp.concatenate([x, blank[1]], axis=0) for x in thirds(loads))
    return lax.dot_general(
        jnp.concatenate([a, a, b, b, a, c], axis=0).astype(BF16),
        jnp.concatenate([d, e, d, e, f, d], axis=0).astype(BF16),
        (((0,), (0,)), ((), ())),
        preferred_element_type=F32,
    )


def strain_of(own, before, after, neighbours_ref):
    points = own.shape[1]
    place = lax.broadcasted_iota(jnp.int32, own.shape, 1)
    left = jnp.where(place == 0, before, pltpu.roll(own, 1, 1))
    right = jnp.where(place == points - 1, after, pltpu.roll(own, points - 1, 1))
    first, second = neighbours_ref[0:1, :], neighbours_ref[1:2, :]
    lower = jnp.where(first == place, left, own)
    upper = jnp.where(second == place + 2, right, own)
    return (upper - lower) / (second - first).astype(F32)


def elastic_kernel(
    per_point,
    pick_ref,
    field_ref,
    neighbours_ref,
    loads_ref,
    stiffness_ref,
    state_ref,
    elastic_ref,
    sum_ref,
    point_ref,
):
    own = stack_rows(field_ref)
    points = own.shape[1]
    modes = state_ref.shape[2]
    tile = TILE * per_point
    strain = strain_of(own, jnp.zeros_like(own), jnp.zeros_like(own), neighbours_ref)
    load = spread(strain, stack_rows(loads_ref))
    stiffness = stiffness_ref[0]
    shift = dot(jnp.concatenate(halves(load), axis=0), stiffness)
    point_ref[...] = shift[:points, :] + shift[points:, :]
    for t in range(points // TILE):
        span, at = slice(t * tile, (t + 1) * tile), slice(t * TILE, (t + 1) * TILE)
        acc = dot(state_ref[0, span, :], stiffness)
        acc = acc.reshape(TILE, per_point, modes) + point_ref[at, :][:, None, :]
        elastic_ref[span, :] = acc.reshape(tile, modes).astype(BF16)
        sum_ref[at, :] = dot(pick_ref[...], elastic_ref[span, :])


def plastic_kernel(
    per_point,
    width,
    route_ref,
    core_ref,
    chip_ref,
    field_ref,
    neighbours_ref,
    loads_ref,
    stiffness_ref,
    state_ref,
    expand_ref,
    contract_ref,
    flags_ref,
    readout_ref,
    force_ref,
    elastic_ref,
    start_ref,
    out_ref,
    residual_ref,
    next_ref,
    list_ref,
    sum_ref,
    edge_ref,
    hidden_ref,
    bulk_sem,
    edge_sems,
):
    rows, modes = elastic_ref.shape
    points = rows // per_point
    batches = rows // BATCH
    edge = EDGE * per_point
    middle = slice(edge, rows - edge)
    bulk = pltpu.make_async_copy(elastic_ref.at[middle, :], out_ref.at[0, middle, :], bulk_sem)
    bulk.start()
    count = list_alive(route_ref, list_ref, batches)

    odd = lax.axis_index("sub") % 2 == 1
    own, core, chip = stack_rows(field_ref), stack_rows(core_ref), stack_rows(chip_ref)
    before = pltpu.roll(jnp.where(odd, core, chip), 1, 1)
    after = pltpu.roll(jnp.where(odd, chip, core), points - 1, 1)
    strain = strain_of(own, before, after, neighbours_ref)
    loads = stack_rows(loads_ref)
    near = [p % points for p in range(-EDGE, EDGE)]
    near = near[EDGE:] + near[:EDGE]
    load = jnp.concatenate(
        [jnp.sum(strain[:, p : p + 1] * loads, axis=0, keepdims=True) for p in near], axis=0
    )
    high, low = halves(load)
    blank = jnp.zeros((GROUP, modes), F32)
    extra = jnp.concatenate([high.astype(F32), low.astype(F32), blank], axis=0).astype(BF16)
    ends = [slice(0, edge), slice(rows - edge, rows)]
    acc = dot(
        jnp.concatenate([state_ref[0, s, :] for s in ends] + [extra], axis=0), stiffness_ref[0]
    )
    shift = acc[2 * edge : 2 * edge + 2 * EDGE, :] + acc[2 * edge + 2 * EDGE : 2 * edge + 4 * EDGE, :]
    fixed = acc[: 2 * edge, :].reshape(2 * EDGE, per_point, modes) + shift[:, None, :]
    fixed = fixed.reshape(2 * edge, modes).astype(BF16)
    edge_ref[...] = fixed
    totals = jnp.sum(fixed.astype(F32).reshape(2 * EDGE, per_point, modes), axis=1)
    sum_ref[...] = start_ref[...]
    sum_ref[0:EDGE, :] = totals[:EDGE, :]
    sum_ref[points - EDGE : points, :] = totals[EDGE:, :]
    edges = [
        pltpu.make_async_copy(edge_ref.at[i * edge : (i + 1) * edge, :], out_ref.at[0, s, :], edge_sems.at[i])
        for i, s in enumerate(ends)
    ]
    for copy in edges:
        copy.start()

    def chunk(c):
        chosen = [list_ref[jnp.maximum(jnp.minimum(c * width + j, count - 1), 0)] for j in range(width)]
        starts = [pl.multiple_of(b * BATCH, BATCH) for b in chosen]
        parts = []
        for b, s in zip(chosen, starts):
            part = elastic_ref[pl.ds(s, BATCH), :]
            parts.append(jnp.where(b == 0, fixed[:edge, :], part[:edge, :]))
            parts.append(part[edge : BATCH - edge, :])
            parts.append(jnp.where(b == batches - 1, fixed[edge:, :], part[BATCH - edge :, :]))
        taken = jnp.concatenate(parts, axis=0)
        for h in range(0, expand_ref.shape[2], 512):
            hidden_ref[:, h : h + 512] = silu(dot(taken, expand_ref[0, :, h : h + 512])).astype(BF16)
        correction = dot(hidden_ref[...], contract_ref[0])
        p = lax.broadcasted_iota(jnp.int32, (points, BATCH), 0) * per_point
        r = lax.broadcasted_iota(jnp.int32, (points, BATCH), 1)
        owners, changes = [], []
        for j, s in enumerate(starts):
            at = slice(j * BATCH, (j + 1) * BATCH)
            flags = flags_ref[0:1, pl.ds(s, BATCH)].astype(F32)
            column = jnp.broadcast_to(flags, (BATCH, BATCH)).T
            column = jnp.concatenate([column] * (modes // BATCH), axis=1)
            change = column * correction[at, :]
            slot = pl.multiple_of((c * width + j) * BATCH, BATCH)
            next_ref[pl.ds(slot, BATCH), :] = (taken[at, :].astype(F32) + change).astype(BF16)
            row = r + jnp.where(c * width + j < count, s, -rows)
            owners.append(jnp.where((row >= p) & (row < p + per_point), 1.0, 0.0).astype(BF16))
            changes.append(change.astype(BF16))
        sum_ref[...] += dot(jnp.concatenate(owners, axis=1), jnp.concatenate(changes, axis=0))

    pl.loop(0, (count + width - 1) // width)(chunk)

    readout = jnp.broadcast_to(readout_ref[...], (GROUP, modes))
    parts = dot_nt(readout, jnp.concatenate(halves(sum_ref[...]), axis=0))[0:1, :]
    mean = (parts[:, :points] + parts[:, points:]) * (1.0 / per_point)
    residual_ref[...] = (force_ref[...] - mean).astype(BF16)
    for copy in [bulk] + edges:
        copy.wait()


def write_kernel(route_ref, next_ref, states_ref, out_ref, list_ref, sem):
    del states_ref
    count = list_alive(route_ref, list_ref, route_ref.shape[2])

    def changed(i):
        source = pl.ds(pl.multiple_of(i * BATCH, BATCH), BATCH)
        target = pl.ds(pl.multiple_of(list_ref[i] * BATCH, BATCH), BATCH)
        return pltpu.make_async_copy(next_ref.at[source, :], out_ref.at[0, target, :], sem)

    @pl.loop(0, count)
    def _(i):
        changed(i).start()

    @pl.loop(0, count)
    def _(i):
        changed(i).wait()


def pick_kernel(per_point, pick_ref):
    shape = pick_ref.shape
    p = lax.broadcasted_iota(jnp.int32, shape, 0)
    r = lax.broadcasted_iota(jnp.int32, shape, 1)
    pick_ref[...] = jnp.where((r >= p * per_point) & (r < (p + 1) * per_point), 1.0, 0.0).astype(BF16)


def coarse_kernel(inverse_ref, *refs):
    pairs, out_ref = refs[:-1], refs[-1]
    points = out_ref.shape[1]
    me = lax.axis_index("sub")
    values, columns = [], []
    for k, pair_ref in enumerate(pairs):
        chip = (me // 2) ^ k
        for c in range(2):
            block = pl.multiple_of((2 * chip + (me + c) % 2) * points, points)
            values.append(jnp.broadcast_to(pair_ref[c : c + 1, :], (GROUP, points)))
            columns.append(inverse_ref[0, :, pl.ds(block, points)])
    total = dot_nt(jnp.concatenate(values, axis=1), jnp.concatenate(columns, axis=1))
    out_ref[...] = total[0:1, :]


def swap_pairs(n, offset):
    pairs = [(i, i + 1) for i in range(offset, n - 1, 2)]
    return pairs + [(j, i) for i, j in pairs]


def on_device(
    displacement,
    neighbours,
    micro_state,
    strain_loads,
    stiffness,
    expand_weight,
    contract_weight,
    batch_route,
    yield_flags,
    readout,
    external_force,
    coarse_inverse,
):
    n = lax.axis_size("sub")
    points = displacement.shape[2]
    rows, modes = micro_state.shape[1:]
    hidden_size = expand_weight.shape[2]
    per_point = rows // points
    batches = rows // BATCH
    reach = min(16, n // 2, batches)
    width = min(4, reach)
    slots = -(-reach // width) * width
    field = jnp.transpose(displacement, (1, 0, 2))
    loads = jnp.transpose(strain_loads, (1, 0, 2))
    vmem = pl.BlockSpec(memory_space=pltpu.VMEM)
    smem = pl.BlockSpec(memory_space=pltpu.SMEM)
    hbm = pl.BlockSpec(memory_space=pltpu.HBM)
    pick = pl.pallas_call(
        functools.partial(pick_kernel, per_point),
        out_shape=jax.ShapeDtypeStruct((TILE, TILE * per_point), BF16),
        out_specs=vmem,
        compiler_params=pltpu.CompilerParams(vmem_limit_bytes=MIB),
        cost_estimate=pl.CostEstimate(flops=20 * 10**9, bytes_accessed=MIB, transcendentals=0),
    )()
    from_core = lax.ppermute(field, "sub", swap_pairs(n, 0))
    from_chip = lax.ppermute(field, "sub", swap_pairs(n, 1))
    elastic, sums = pl.pallas_call(
        functools.partial(elastic_kernel, per_point),
        out_shape=(
            jax.ShapeDtypeStruct((rows, modes), BF16),
            jax.ShapeDtypeStruct((points, modes), F32),
        ),
        in_specs=[vmem] * 6,
        out_specs=(vmem, vmem),
        scratch_shapes=[pltpu.VMEM((points, modes), F32)],
        compiler_params=pltpu.CompilerParams(vmem_limit_bytes=20 * MIB),
        cost_estimate=pl.CostEstimate(
            flops=2 * rows * modes * modes, bytes_accessed=8 * MIB, transcendentals=0
        ),
    )(pick, field, neighbours, loads, stiffness, micro_state)
    states, residual, updated = pl.pallas_call(
        functools.partial(plastic_kernel, per_point, width),
        out_shape=(
            jax.ShapeDtypeStruct((1, rows, modes), BF16),
            jax.ShapeDtypeStruct((1, points), BF16),
            jax.ShapeDtypeStruct((slots * BATCH, modes), BF16),
        ),
        in_specs=[smem] + [vmem] * 14,
        out_specs=(hbm, vmem, vmem),
        scratch_shapes=[
            pltpu.SMEM((batches + 1,), jnp.int32),
            pltpu.VMEM((points, modes), F32),
            pltpu.VMEM((2 * EDGE * per_point, modes), BF16),
            pltpu.VMEM((width * BATCH, hidden_size), BF16),
            pltpu.SemaphoreType.DMA(()),
            pltpu.SemaphoreType.DMA((2,)),
        ],
        compiler_params=pltpu.CompilerParams(vmem_limit_bytes=28 * MIB),
        cost_estimate=pl.CostEstimate(
            flops=4 * width * BATCH * modes * hidden_size, bytes_accessed=8 * MIB, transcendentals=0
        ),
    )(
        batch_route,
        from_core,
        from_chip,
        field,
        neighbours,
        loads,
        stiffness,
        micro_state,
        expand_weight,
        contract_weight,
        yield_flags,
        readout,
        external_force,
        elastic,
        sums,
    )
    states_next = pl.pallas_call(
        write_kernel,
        out_shape=jax.ShapeDtypeStruct((1, rows, modes), BF16),
        in_specs=[smem, vmem, hbm],
        out_specs=hbm,
        scratch_shapes=[pltpu.SMEM((batches + 1,), jnp.int32), pltpu.SemaphoreType.DMA(())],
        input_output_aliases={2: 0},
        compiler_params=pltpu.CompilerParams(vmem_limit_bytes=4 * MIB),
        cost_estimate=pl.CostEstimate(flops=0, bytes_accessed=2 * MIB, transcendentals=0),
    )(batch_route, updated, states)
    if n // 2 > NEAR_CHIPS:
        everyone = lax.all_gather(residual, "sub", axis=1, tiled=True)[0]
        return states_next, dot(coarse_inverse[0], everyone)[None]
    other = lax.ppermute(residual, "sub", swap_pairs(n, 0))
    pair = jnp.concatenate([residual, other], axis=0)
    pairs = [pair] + [
        lax.ppermute(pair, "sub", [(i, i ^ (2 * k)) for i in range(n)]) for k in range(1, n // 2)
    ]
    coarse = pl.pallas_call(
        coarse_kernel,
        out_shape=jax.ShapeDtypeStruct((1, points), F32),
        in_specs=[vmem] * (1 + len(pairs)),
        out_specs=vmem,
        compiler_params=pltpu.CompilerParams(vmem_limit_bytes=4 * MIB),
    )(coarse_inverse, *pairs)
    return (states_next, coarse)


def solution(mesh):
    return jax.shard_map(
        on_device,
        mesh=mesh,
        in_specs=(
            P("variant", None, "sub"),
            P(None, "sub"),
            P("variant", "sub", None),
            P("variant", None, None),
            P("variant", None, None),
            P("variant", None, None),
            P("variant", None, None),
            P("variant", None, "sub"),
            P("variant", "sub"),
            P("variant", None),
            P("variant", "sub"),
            P("variant", "sub", None),
        ),
        out_specs=(P("variant", "sub", None), P("variant", "sub")),
        check_vma=False,
    )
```

```python
import functools

import jax
import jax.numpy as jnp
from jax import lax
from jax.experimental import pallas as pl
from jax.experimental.pallas import tpu as pltpu
from jax.sharding import PartitionSpec as P

BATCH = 128
GROUP = 8
TILE = 32
EDGE = 2
NEAR_CHIPS = 4
MIB = 1 << 20
F32 = jnp.float32
BF16 = jnp.bfloat16
NT = (((1,), (1,)), ((), ()))


def dot(a, b):
    return jnp.dot(a, b, preferred_element_type=F32)


def dot_nt(a, b, precision=None):
    return lax.dot_general(a, b, NT, precision=precision, preferred_element_type=F32)


def halves(x):
    high = x.astype(BF16)
    return high, (x - high.astype(F32)).astype(BF16)


def silu(a):
    half = 0.5 * a
    return half + half * jnp.tanh(half)


def list_alive(route_ref, list_ref, batches):
    count = jnp.int32(0)
    for b in range(batches):
        list_ref[count] = jnp.int32(b)
        count = count + (route_ref[0, 0, b] >= 0).astype(jnp.int32)
    return count


def stack_rows(ref):
    return jnp.concatenate([ref[k] for k in range(ref.shape[0])], axis=0)


def thirds(x):
    high = x.astype(BF16).astype(F32)
    middle = (x - high).astype(BF16).astype(F32)
    return high, middle, x - high - middle


def spread(strain, loads):
    blank = [jnp.zeros((GROUP - strain.shape[0] % GROUP, x.shape[1]), F32) for x in (strain, loads)]
    a, b, c = (jnp.concatenate([x, blank[0]], axis=0) for x in thirds(strain))
    d, e, f = (jnp.concatenate([x, blank[1]], axis=0) for x in thirds(loads))
    return lax.dot_general(
        jnp.concatenate([a, a, b, b, a, c], axis=0).astype(BF16),
        jnp.concatenate([d, e, d, e, f, d], axis=0).astype(BF16),
        (((0,), (0,)), ((), ())),
        preferred_element_type=F32,
    )


def strain_of(own, before, after, neighbours_ref):
    points = own.shape[1]
    place = lax.broadcasted_iota(jnp.int32, own.shape, 1)
    left = jnp.where(place == 0, before, pltpu.roll(own, 1, 1))
    right = jnp.where(place == points - 1, after, pltpu.roll(own, points - 1, 1))
    first, second = neighbours_ref[0:1, :], neighbours_ref[1:2, :]
    lower = jnp.where(first == place, left, own)
    upper = jnp.where(second == place + 2, right, own)
    return (upper - lower) / (second - first).astype(F32)


def elastic_kernel(
    per_point,
    blank_ref,
    field_ref,
    neighbours_ref,
    loads_ref,
    stiffness_ref,
    state_ref,
    elastic_ref,
    sum_ref,
    point_ref,
):
    own = stack_rows(field_ref)
    points = own.shape[1]
    modes = state_ref.shape[2]
    tile = TILE * per_point
    strain = strain_of(own, blank_ref[...], blank_ref[...], neighbours_ref)
    load = spread(strain, stack_rows(loads_ref))
    stiffness = stiffness_ref[0]
    shift = dot(jnp.concatenate(halves(load), axis=0), stiffness)
    point_ref[...] = shift[:points, :] + shift[points:, :]
    for t in range(points // TILE):
        span, at = slice(t * tile, (t + 1) * tile), slice(t * TILE, (t + 1) * TILE)
        acc = dot(state_ref[0, span, :], stiffness)
        acc = acc.reshape(TILE, per_point, modes) + point_ref[at, :][:, None, :]
        elastic_ref[span, :] = acc.reshape(tile, modes).astype(BF16)
        sum_ref[at, :] = jnp.sum(acc, axis=1)


def plastic_kernel(
    per_point,
    width,
    route_ref,
    core_ref,
    chip_ref,
    field_ref,
    neighbours_ref,
    loads_ref,
    stiffness_ref,
    state_ref,
    expand_ref,
    contract_ref,
    flags_ref,
    readout_ref,
    force_ref,
    elastic_ref,
    start_ref,
    out_ref,
    residual_ref,
    next_ref,
    list_ref,
    sum_ref,
    edge_ref,
    hidden_ref,
    bulk_sem,
    edge_sems,
):
    rows, modes = elastic_ref.shape
    points = rows // per_point
    batches = rows // BATCH
    edge = EDGE * per_point
    middle = slice(edge, rows - edge)
    bulk = pltpu.make_async_copy(elastic_ref.at[middle, :], out_ref.at[0, middle, :], bulk_sem)
    bulk.start()
    count = list_alive(route_ref, list_ref, batches)

    odd = lax.axis_index("sub") % 2 == 1
    own, core, chip = stack_rows(field_ref), stack_rows(core_ref), stack_rows(chip_ref)
    before = pltpu.roll(jnp.where(odd, core, chip), 1, 1)
    after = pltpu.roll(jnp.where(odd, chip, core), points - 1, 1)
    strain = strain_of(own, before, after, neighbours_ref)
    loads = stack_rows(loads_ref)
    near = [p % points for p in range(-EDGE, EDGE)]
    near = near[EDGE:] + near[:EDGE]
    load = jnp.concatenate(
        [jnp.sum(strain[:, p : p + 1] * loads, axis=0, keepdims=True) for p in near], axis=0
    )
    high, low = halves(load)
    blank = jnp.zeros((GROUP, modes), F32)
    extra = jnp.concatenate([high.astype(F32), low.astype(F32), blank], axis=0).astype(BF16)
    ends = [slice(0, edge), slice(rows - edge, rows)]
    acc = dot(
        jnp.concatenate([state_ref[0, s, :] for s in ends] + [extra], axis=0), stiffness_ref[0]
    )
    shift = acc[2 * edge : 2 * edge + 2 * EDGE, :] + acc[2 * edge + 2 * EDGE : 2 * edge + 4 * EDGE, :]
    fixed = acc[: 2 * edge, :].reshape(2 * EDGE, per_point, modes) + shift[:, None, :]
    fixed = fixed.reshape(2 * edge, modes).astype(BF16)
    edge_ref[...] = fixed
    totals = jnp.sum(fixed.astype(F32).reshape(2 * EDGE, per_point, modes), axis=1)
    sum_ref[...] = start_ref[...]
    sum_ref[0:EDGE, :] = totals[:EDGE, :]
    sum_ref[points - EDGE : points, :] = totals[EDGE:, :]
    edges = [
        pltpu.make_async_copy(edge_ref.at[i * edge : (i + 1) * edge, :], out_ref.at[0, s, :], edge_sems.at[i])
        for i, s in enumerate(ends)
    ]
    for copy in edges:
        copy.start()

    def chunk(c):
        chosen = [list_ref[jnp.maximum(jnp.minimum(c * width + j, count - 1), 0)] for j in range(width)]
        starts = [pl.multiple_of(b * BATCH, BATCH) for b in chosen]
        parts = []
        for b, s in zip(chosen, starts):
            part = elastic_ref[pl.ds(s, BATCH), :]
            parts.append(jnp.where(b == 0, fixed[:edge, :], part[:edge, :]))
            parts.append(part[edge : BATCH - edge, :])
            parts.append(jnp.where(b == batches - 1, fixed[edge:, :], part[BATCH - edge :, :]))
        taken = jnp.concatenate(parts, axis=0)
        for h in range(0, expand_ref.shape[2], 512):
            hidden_ref[:, h : h + 512] = silu(dot(taken, expand_ref[0, :, h : h + 512])).astype(BF16)
        correction = dot(hidden_ref[...], contract_ref[0])
        p = lax.broadcasted_iota(jnp.int32, (points, BATCH), 0) * per_point
        r = lax.broadcasted_iota(jnp.int32, (points, BATCH), 1)
        owners, changes = [], []
        for j, s in enumerate(starts):
            at = slice(j * BATCH, (j + 1) * BATCH)
            flags = flags_ref[0:1, pl.ds(s, BATCH)].astype(F32)
            column = jnp.broadcast_to(flags, (BATCH, BATCH)).T
            column = jnp.concatenate([column] * (modes // BATCH), axis=1)
            change = column * correction[at, :]
            slot = pl.multiple_of((c * width + j) * BATCH, BATCH)
            next_ref[pl.ds(slot, BATCH), :] = (taken[at, :].astype(F32) + change).astype(BF16)
            row = r + jnp.where(c * width + j < count, s, -rows)
            owners.append(jnp.where((row >= p) & (row < p + per_point), 1.0, 0.0).astype(BF16))
            changes.append(change.astype(BF16))
        sum_ref[...] += dot(jnp.concatenate(owners, axis=1), jnp.concatenate(changes, axis=0))

    pl.loop(0, (count + width - 1) // width)(chunk)

    readout = jnp.broadcast_to(readout_ref[...], (GROUP, modes))
    parts = dot_nt(readout, jnp.concatenate(halves(sum_ref[...]), axis=0))[0:1, :]
    mean = (parts[:, :points] + parts[:, points:]) * (1.0 / per_point)
    residual_ref[...] = (force_ref[...] - mean).astype(BF16)
    for copy in [bulk] + edges:
        copy.wait()


def write_kernel(route_ref, next_ref, states_ref, out_ref, list_ref, sem):
    del states_ref
    count = list_alive(route_ref, list_ref, route_ref.shape[2])

    def changed(i):
        source = pl.ds(pl.multiple_of(i * BATCH, BATCH), BATCH)
        target = pl.ds(pl.multiple_of(list_ref[i] * BATCH, BATCH), BATCH)
        return pltpu.make_async_copy(next_ref.at[source, :], out_ref.at[0, target, :], sem)

    @pl.loop(0, count)
    def _(i):
        changed(i).start()

    @pl.loop(0, count)
    def _(i):
        changed(i).wait()


def blank_kernel(blank_ref):
    blank_ref[...] = jnp.zeros_like(blank_ref)


def coarse_kernel(inverse_ref, *refs):
    pairs, out_ref = refs[:-1], refs[-1]
    points = out_ref.shape[1]
    me = lax.axis_index("sub")
    values, columns = [], []
    for k, pair_ref in enumerate(pairs):
        chip = (me // 2) ^ k
        for c in range(2):
            block = pl.multiple_of((2 * chip + (me + c) % 2) * points, points)
            values.append(jnp.broadcast_to(pair_ref[c : c + 1, :], (GROUP, points)))
            columns.append(inverse_ref[0, :, pl.ds(block, points)])
    total = dot_nt(jnp.concatenate(values, axis=1), jnp.concatenate(columns, axis=1))
    out_ref[...] = total[0:1, :]


def swap_pairs(n, offset):
    pairs = [(i, i + 1) for i in range(offset, n - 1, 2)]
    return pairs + [(j, i) for i, j in pairs]


def on_device(
    displacement,
    neighbours,
    micro_state,
    strain_loads,
    stiffness,
    expand_weight,
    contract_weight,
    batch_route,
    yield_flags,
    readout,
    external_force,
    coarse_inverse,
):
    n = lax.axis_size("sub")
    points = displacement.shape[2]
    rows, modes = micro_state.shape[1:]
    hidden_size = expand_weight.shape[2]
    per_point = rows // points
    batches = rows // BATCH
    reach = min(16, n // 2, batches)
    width = min(4, reach)
    slots = -(-reach // width) * width
    field = jnp.transpose(displacement, (1, 0, 2))
    loads = jnp.transpose(strain_loads, (1, 0, 2))
    vmem = pl.BlockSpec(memory_space=pltpu.VMEM)
    smem = pl.BlockSpec(memory_space=pltpu.SMEM)
    hbm = pl.BlockSpec(memory_space=pltpu.HBM)
    blank = pl.pallas_call(
        blank_kernel,
        out_shape=jax.ShapeDtypeStruct((displacement.shape[1], points), F32),
        out_specs=vmem,
        compiler_params=pltpu.CompilerParams(vmem_limit_bytes=MIB),
        cost_estimate=pl.CostEstimate(flops=20 * 10**9, bytes_accessed=MIB, transcendentals=0),
    )()
    from_core = lax.ppermute(field, "sub", swap_pairs(n, 0))
    from_chip = lax.ppermute(field, "sub", swap_pairs(n, 1))
    elastic, sums = pl.pallas_call(
        functools.partial(elastic_kernel, per_point),
        out_shape=(
            jax.ShapeDtypeStruct((rows, modes), BF16),
            jax.ShapeDtypeStruct((points, modes), F32),
        ),
        in_specs=[vmem] * 6,
        out_specs=(vmem, vmem),
        scratch_shapes=[pltpu.VMEM((points, modes), F32)],
        compiler_params=pltpu.CompilerParams(vmem_limit_bytes=20 * MIB),
        cost_estimate=pl.CostEstimate(
            flops=2 * rows * modes * modes, bytes_accessed=8 * MIB, transcendentals=0
        ),
    )(blank, field, neighbours, loads, stiffness, micro_state)
    states, residual, updated = pl.pallas_call(
        functools.partial(plastic_kernel, per_point, width),
        out_shape=(
            jax.ShapeDtypeStruct((1, rows, modes), BF16),
            jax.ShapeDtypeStruct((1, points), BF16),
            jax.ShapeDtypeStruct((slots * BATCH, modes), BF16),
        ),
        in_specs=[smem] + [vmem] * 14,
        out_specs=(hbm, vmem, vmem),
        scratch_shapes=[
            pltpu.SMEM((batches + 1,), jnp.int32),
            pltpu.VMEM((points, modes), F32),
            pltpu.VMEM((2 * EDGE * per_point, modes), BF16),
            pltpu.VMEM((width * BATCH, hidden_size), BF16),
            pltpu.SemaphoreType.DMA(()),
            pltpu.SemaphoreType.DMA((2,)),
        ],
        compiler_params=pltpu.CompilerParams(vmem_limit_bytes=28 * MIB),
        cost_estimate=pl.CostEstimate(
            flops=4 * width * BATCH * modes * hidden_size, bytes_accessed=8 * MIB, transcendentals=0
        ),
    )(
        batch_route,
        from_core,
        from_chip,
        field,
        neighbours,
        loads,
        stiffness,
        micro_state,
        expand_weight,
        contract_weight,
        yield_flags,
        readout,
        external_force,
        elastic,
        sums,
    )
    states_next = pl.pallas_call(
        write_kernel,
        out_shape=jax.ShapeDtypeStruct((1, rows, modes), BF16),
        in_specs=[smem, vmem, hbm],
        out_specs=hbm,
        scratch_shapes=[pltpu.SMEM((batches + 1,), jnp.int32), pltpu.SemaphoreType.DMA(())],
        input_output_aliases={2: 0},
        compiler_params=pltpu.CompilerParams(vmem_limit_bytes=4 * MIB),
        cost_estimate=pl.CostEstimate(flops=0, bytes_accessed=2 * MIB, transcendentals=0),
    )(batch_route, updated, states)
    if n // 2 > NEAR_CHIPS:
        everyone = lax.all_gather(residual, "sub", axis=1, tiled=True)[0]
        return states_next, dot(coarse_inverse[0], everyone)[None]
    other = lax.ppermute(residual, "sub", swap_pairs(n, 0))
    pair = jnp.concatenate([residual, other], axis=0)
    pairs = [pair] + [
        lax.ppermute(pair, "sub", [(i, i ^ (2 * k)) for i in range(n)]) for k in range(1, n // 2)
    ]
    coarse = pl.pallas_call(
        coarse_kernel,
        out_shape=jax.ShapeDtypeStruct((1, points), F32),
        in_specs=[vmem] * (1 + len(pairs)),
        out_specs=vmem,
        compiler_params=pltpu.CompilerParams(vmem_limit_bytes=4 * MIB),
    )(coarse_inverse, *pairs)
    return (states_next, coarse)


def solution(mesh):
    return jax.shard_map(
        on_device,
        mesh=mesh,
        in_specs=(
            P("variant", None, "sub"),
            P(None, "sub"),
            P("variant", "sub", None),
            P("variant", None, None),
            P("variant", None, None),
            P("variant", None, None),
            P("variant", None, None),
            P("variant", None, "sub"),
            P("variant", "sub"),
            P("variant", None),
            P("variant", "sub"),
            P("variant", "sub", None),
        ),
        out_specs=(P("variant", "sub", None), P("variant", "sub")),
        check_vma=False,
    )
```

```python
import functools

import jax
import jax.numpy as jnp
from jax import lax
from jax.experimental import pallas as pl
from jax.experimental.pallas import tpu as pltpu
from jax.sharding import PartitionSpec as P

BATCH = 128
GROUP = 8
TILE = 32
EDGE = 2
NEAR_CHIPS = 4
MIB = 1 << 20
F32 = jnp.float32
BF16 = jnp.bfloat16
NT = (((1,), (1,)), ((), ()))


def dot(a, b):
    return jnp.dot(a, b, preferred_element_type=F32)


def dot_nt(a, b, precision=None):
    return lax.dot_general(a, b, NT, precision=precision, preferred_element_type=F32)


def halves(x):
    high = x.astype(BF16)
    return high, (x - high.astype(F32)).astype(BF16)


def silu(a):
    half = 0.5 * a
    return half + half * jnp.tanh(half)


def list_alive(route_ref, list_ref, batches):
    count = jnp.int32(0)
    for b in range(batches):
        list_ref[count] = jnp.int32(b)
        count = count + (route_ref[0, 0, b] >= 0).astype(jnp.int32)
    return count


def stack_rows(ref):
    return jnp.concatenate([ref[k] for k in range(ref.shape[0])], axis=0)


def thirds(x):
    high = x.astype(BF16).astype(F32)
    middle = (x - high).astype(BF16).astype(F32)
    return high, middle, x - high - middle


def spread(strain, loads):
    blank = [jnp.zeros((GROUP - strain.shape[0] % GROUP, x.shape[1]), F32) for x in (strain, loads)]
    a, b, c = (jnp.concatenate([x, blank[0]], axis=0) for x in thirds(strain))
    d, e, f = (jnp.concatenate([x, blank[1]], axis=0) for x in thirds(loads))
    return lax.dot_general(
        jnp.concatenate([a, a, b, b, a, c], axis=0).astype(BF16),
        jnp.concatenate([d, e, d, e, f, d], axis=0).astype(BF16),
        (((0,), (0,)), ((), ())),
        preferred_element_type=F32,
    )


def strain_of(own, before, after, neighbours_ref):
    points = own.shape[1]
    place = lax.broadcasted_iota(jnp.int32, own.shape, 1)
    left = jnp.where(place == 0, before, pltpu.roll(own, 1, 1))
    right = jnp.where(place == points - 1, after, pltpu.roll(own, points - 1, 1))
    first, second = neighbours_ref[0:1, :], neighbours_ref[1:2, :]
    lower = jnp.where(first == place, left, own)
    upper = jnp.where(second == place + 2, right, own)
    return (upper - lower) / (second - first).astype(F32)


def elastic_kernel(
    per_point,
    blank_ref,
    field_ref,
    neighbours_ref,
    loads_ref,
    stiffness_ref,
    state_ref,
    elastic_ref,
    sum_ref,
    end_ref,
    mode_ref,
    point_ref,
):
    own = stack_rows(field_ref)
    points = own.shape[1]
    modes = state_ref.shape[2]
    tile = TILE * per_point
    strain = strain_of(own, blank_ref[...], blank_ref[...], neighbours_ref)
    loads = stack_rows(loads_ref)
    load = spread(strain, loads)
    loads = jnp.concatenate([loads, jnp.zeros((mode_ref.shape[0] - loads.shape[0], modes), F32)], axis=0)
    stiffness = stiffness_ref[0]
    high, low = halves(jnp.concatenate([load, loads], axis=0))
    shift = dot(high, stiffness) + dot(low, stiffness)
    point_ref[...] = shift[:points, :]
    mode_ref[...] = shift[points:, :]
    tiles = points // TILE
    edge = end_ref.shape[0] // 2
    for t in range(tiles):
        span, at = slice(t * tile, (t + 1) * tile), slice(t * TILE, (t + 1) * TILE)
        acc = dot(state_ref[0, span, :], stiffness)
        acc = acc.reshape(TILE, per_point, modes) + point_ref[at, :][:, None, :]
        elastic_ref[span, :] = acc.reshape(tile, modes).astype(BF16)
        sum_ref[at, :] = jnp.sum(acc, axis=1)
        if t == 0:
            end_ref[:edge, :] = acc.reshape(tile, modes)[:edge, :]
        if t == tiles - 1:
            end_ref[edge:, :] = acc.reshape(tile, modes)[tile - edge :, :]


def plastic_kernel(
    per_point,
    width,
    route_ref,
    core_ref,
    chip_ref,
    field_ref,
    neighbours_ref,
    expand_ref,
    contract_ref,
    flags_ref,
    readout_ref,
    force_ref,
    elastic_ref,
    start_ref,
    end_ref,
    mode_ref,
    out_ref,
    residual_ref,
    next_ref,
    list_ref,
    sum_ref,
    edge_ref,
    hidden_ref,
    bulk_sem,
    edge_sems,
):
    rows, modes = elastic_ref.shape
    points = rows // per_point
    batches = rows // BATCH
    edge = EDGE * per_point
    middle = slice(edge, rows - edge)
    bulk = pltpu.make_async_copy(elastic_ref.at[middle, :], out_ref.at[0, middle, :], bulk_sem)
    bulk.start()
    count = list_alive(route_ref, list_ref, batches)

    odd = lax.axis_index("sub") % 2 == 1
    own, core, chip = stack_rows(field_ref), stack_rows(core_ref), stack_rows(chip_ref)
    before = pltpu.roll(jnp.where(odd, core, chip), 1, 1)
    after = pltpu.roll(jnp.where(odd, chip, core), points - 1, 1)
    blank = jnp.zeros_like(own)
    change = strain_of(own, before, after, neighbours_ref) - strain_of(own, blank, blank, neighbours_ref)
    shifts = [
        jnp.sum(change[:, p : p + 1] * mode_ref[: own.shape[0], :], axis=0, keepdims=True)
        for p in (0, points - 1)
    ]
    ends = [slice(0, edge), slice(rows - edge, rows)]
    fixed = jnp.concatenate(
        [
            end_ref[:per_point, :] + shifts[0],
            end_ref[per_point : 2 * edge - per_point, :],
            end_ref[2 * edge - per_point :, :] + shifts[1],
        ],
        axis=0,
    ).astype(BF16)
    edge_ref[...] = fixed
    sum_ref[...] = start_ref[...]
    sum_ref[0:1, :] = start_ref[0:1, :] + per_point * shifts[0]
    sum_ref[points - 1 : points, :] = start_ref[points - 1 : points, :] + per_point * shifts[1]
    edges = [
        pltpu.make_async_copy(edge_ref.at[i * edge : (i + 1) * edge, :], out_ref.at[0, s, :], edge_sems.at[i])
        for i, s in enumerate(ends)
    ]
    for copy in edges:
        copy.start()

    def chunk(c):
        chosen = [list_ref[jnp.maximum(jnp.minimum(c * width + j, count - 1), 0)] for j in range(width)]
        starts = [pl.multiple_of(b * BATCH, BATCH) for b in chosen]
        parts = []
        for b, s in zip(chosen, starts):
            part = elastic_ref[pl.ds(s, BATCH), :]
            parts.append(jnp.where(b == 0, fixed[:edge, :], part[:edge, :]))
            parts.append(part[edge : BATCH - edge, :])
            parts.append(jnp.where(b == batches - 1, fixed[edge:, :], part[BATCH - edge :, :]))
        taken = jnp.concatenate(parts, axis=0)
        for h in range(0, expand_ref.shape[2], 512):
            hidden_ref[:, h : h + 512] = silu(dot(taken, expand_ref[0, :, h : h + 512])).astype(BF16)
        correction = dot(hidden_ref[...], contract_ref[0])
        p = lax.broadcasted_iota(jnp.int32, (points, BATCH), 0) * per_point
        r = lax.broadcasted_iota(jnp.int32, (points, BATCH), 1)
        owners, changes = [], []
        for j, s in enumerate(starts):
            at = slice(j * BATCH, (j + 1) * BATCH)
            flags = flags_ref[0:1, pl.ds(s, BATCH)].astype(F32)
            column = jnp.broadcast_to(flags, (BATCH, BATCH)).T
            column = jnp.concatenate([column] * (modes // BATCH), axis=1)
            change = column * correction[at, :]
            slot = pl.multiple_of((c * width + j) * BATCH, BATCH)
            next_ref[pl.ds(slot, BATCH), :] = (taken[at, :].astype(F32) + change).astype(BF16)
            row = r + jnp.where(c * width + j < count, s, -rows)
            owners.append(jnp.where((row >= p) & (row < p + per_point), 1.0, 0.0).astype(BF16))
            changes.append(change.astype(BF16))
        sum_ref[...] += dot(jnp.concatenate(owners, axis=1), jnp.concatenate(changes, axis=0))

    pl.loop(0, (count + width - 1) // width)(chunk)

    readout = jnp.broadcast_to(readout_ref[...], (GROUP, modes))
    parts = dot_nt(readout, jnp.concatenate(halves(sum_ref[...]), axis=0))[0:1, :]
    mean = (parts[:, :points] + parts[:, points:]) * (1.0 / per_point)
    residual_ref[...] = (force_ref[...] - mean).astype(BF16)
    for copy in [bulk] + edges:
        copy.wait()


def write_kernel(route_ref, next_ref, states_ref, out_ref, list_ref, sem):
    del states_ref
    count = list_alive(route_ref, list_ref, route_ref.shape[2])

    def changed(i):
        source = pl.ds(pl.multiple_of(i * BATCH, BATCH), BATCH)
        target = pl.ds(pl.multiple_of(list_ref[i] * BATCH, BATCH), BATCH)
        return pltpu.make_async_copy(next_ref.at[source, :], out_ref.at[0, target, :], sem)

    @pl.loop(0, count)
    def _(i):
        changed(i).start()

    @pl.loop(0, count)
    def _(i):
        changed(i).wait()


def blank_kernel(blank_ref):
    blank_ref[...] = jnp.zeros_like(blank_ref)


def coarse_kernel(inverse_ref, *refs):
    pairs, out_ref = refs[:-1], refs[-1]
    points = out_ref.shape[1]
    me = lax.axis_index("sub")
    values, columns = [], []
    for k, pair_ref in enumerate(pairs):
        chip = (me // 2) ^ k
        for c in range(2):
            block = pl.multiple_of((2 * chip + (me + c) % 2) * points, points)
            values.append(jnp.broadcast_to(pair_ref[c : c + 1, :], (GROUP, points)))
            columns.append(inverse_ref[0, :, pl.ds(block, points)])
    total = dot_nt(jnp.concatenate(values, axis=1), jnp.concatenate(columns, axis=1))
    out_ref[...] = total[0:1, :]


def swap_pairs(n, offset):
    pairs = [(i, i + 1) for i in range(offset, n - 1, 2)]
    return pairs + [(j, i) for i, j in pairs]


def on_device(
    displacement,
    neighbours,
    micro_state,
    strain_loads,
    stiffness,
    expand_weight,
    contract_weight,
    batch_route,
    yield_flags,
    readout,
    external_force,
    coarse_inverse,
):
    n = lax.axis_size("sub")
    points = displacement.shape[2]
    rows, modes = micro_state.shape[1:]
    hidden_size = expand_weight.shape[2]
    per_point = rows // points
    batches = rows // BATCH
    reach = min(16, n // 2, batches)
    width = min(4, reach)
    slots = -(-reach // width) * width
    field = jnp.transpose(displacement, (1, 0, 2))
    loads = jnp.transpose(strain_loads, (1, 0, 2))
    vmem = pl.BlockSpec(memory_space=pltpu.VMEM)
    smem = pl.BlockSpec(memory_space=pltpu.SMEM)
    hbm = pl.BlockSpec(memory_space=pltpu.HBM)
    blank = pl.pallas_call(
        blank_kernel,
        out_shape=jax.ShapeDtypeStruct((displacement.shape[1], points), F32),
        out_specs=vmem,
        compiler_params=pltpu.CompilerParams(vmem_limit_bytes=MIB),
        cost_estimate=pl.CostEstimate(flops=20 * 10**9, bytes_accessed=MIB, transcendentals=0),
    )()
    from_core = lax.ppermute(field, "sub", swap_pairs(n, 0))
    from_chip = lax.ppermute(field, "sub", swap_pairs(n, 1))
    edge = EDGE * per_point
    kinds = -(-displacement.shape[1] // GROUP) * GROUP
    elastic, sums, ends, modes_out = pl.pallas_call(
        functools.partial(elastic_kernel, per_point),
        out_shape=(
            jax.ShapeDtypeStruct((rows, modes), BF16),
            jax.ShapeDtypeStruct((points, modes), F32),
            jax.ShapeDtypeStruct((2 * edge, modes), F32),
            jax.ShapeDtypeStruct((kinds, modes), F32),
        ),
        in_specs=[vmem] * 6,
        out_specs=(vmem,) * 4,
        scratch_shapes=[pltpu.VMEM((points, modes), F32)],
        compiler_params=pltpu.CompilerParams(vmem_limit_bytes=20 * MIB),
        cost_estimate=pl.CostEstimate(
            flops=2 * rows * modes * modes, bytes_accessed=8 * MIB, transcendentals=0
        ),
    )(blank, field, neighbours, loads, stiffness, micro_state)
    states, residual, updated = pl.pallas_call(
        functools.partial(plastic_kernel, per_point, width),
        out_shape=(
            jax.ShapeDtypeStruct((1, rows, modes), BF16),
            jax.ShapeDtypeStruct((1, points), BF16),
            jax.ShapeDtypeStruct((slots * BATCH, modes), BF16),
        ),
        in_specs=[smem] + [vmem] * 13,
        out_specs=(hbm, vmem, vmem),
        scratch_shapes=[
            pltpu.SMEM((batches + 1,), jnp.int32),
            pltpu.VMEM((points, modes), F32),
            pltpu.VMEM((2 * EDGE * per_point, modes), BF16),
            pltpu.VMEM((width * BATCH, hidden_size), BF16),
            pltpu.SemaphoreType.DMA(()),
            pltpu.SemaphoreType.DMA((2,)),
        ],
        compiler_params=pltpu.CompilerParams(vmem_limit_bytes=28 * MIB),
        cost_estimate=pl.CostEstimate(
            flops=4 * width * BATCH * modes * hidden_size, bytes_accessed=8 * MIB, transcendentals=0
        ),
    )(
        batch_route,
        from_core,
        from_chip,
        field,
        neighbours,
        expand_weight,
        contract_weight,
        yield_flags,
        readout,
        external_force,
        elastic,
        sums,
        ends,
        modes_out,
    )
    states_next = pl.pallas_call(
        write_kernel,
        out_shape=jax.ShapeDtypeStruct((1, rows, modes), BF16),
        in_specs=[smem, vmem, hbm],
        out_specs=hbm,
        scratch_shapes=[pltpu.SMEM((batches + 1,), jnp.int32), pltpu.SemaphoreType.DMA(())],
        input_output_aliases={2: 0},
        compiler_params=pltpu.CompilerParams(vmem_limit_bytes=4 * MIB),
        cost_estimate=pl.CostEstimate(flops=0, bytes_accessed=2 * MIB, transcendentals=0),
    )(batch_route, updated, states)
    if n // 2 > NEAR_CHIPS:
        everyone = lax.all_gather(residual, "sub", axis=1, tiled=True)[0]
        return states_next, dot(coarse_inverse[0], everyone)[None]
    other = lax.ppermute(residual, "sub", swap_pairs(n, 0))
    pair = jnp.concatenate([residual, other], axis=0)
    pairs = [pair] + [
        lax.ppermute(pair, "sub", [(i, i ^ (2 * k)) for i in range(n)]) for k in range(1, n // 2)
    ]
    coarse = pl.pallas_call(
        coarse_kernel,
        out_shape=jax.ShapeDtypeStruct((1, points), F32),
        in_specs=[vmem] * (1 + len(pairs)),
        out_specs=vmem,
        compiler_params=pltpu.CompilerParams(vmem_limit_bytes=4 * MIB),
    )(coarse_inverse, *pairs)
    return (states_next, coarse)


def solution(mesh):
    return jax.shard_map(
        on_device,
        mesh=mesh,
        in_specs=(
            P("variant", None, "sub"),
            P(None, "sub"),
            P("variant", "sub", None),
            P("variant", None, None),
            P("variant", None, None),
            P("variant", None, None),
            P("variant", None, None),
            P("variant", None, "sub"),
            P("variant", "sub"),
            P("variant", None),
            P("variant", "sub"),
            P("variant", "sub", None),
        ),
        out_specs=(P("variant", "sub", None), P("variant", "sub")),
        check_vma=False,
    )
```

```python
import functools

import jax
import jax.numpy as jnp
from jax import lax
from jax.experimental import pallas as pl
from jax.experimental.pallas import tpu as pltpu
from jax.sharding import PartitionSpec as P

BATCH = 128
GROUP = 16
TILE = 32
EDGE = 2
NEAR_CHIPS = 4
MIB = 1 << 20
F32 = jnp.float32
BF16 = jnp.bfloat16
NT = (((1,), (1,)), ((), ()))


def dot(a, b):
    return jnp.dot(a, b, preferred_element_type=F32)


def dot_nt(a, b, precision=None):
    return lax.dot_general(a, b, NT, precision=precision, preferred_element_type=F32)


def halves(x):
    high = x.astype(BF16)
    return high, (x - high.astype(F32)).astype(BF16)


def silu(a):
    half = 0.5 * a
    return half + half * jnp.tanh(half)


def list_alive(route_ref, list_ref, batches):
    count = jnp.int32(0)
    for b in range(batches):
        list_ref[count] = jnp.int32(b)
        count = count + (route_ref[0, 0, b] >= 0).astype(jnp.int32)
    return count


def stack_rows(ref):
    return jnp.concatenate([ref[k] for k in range(ref.shape[0])], axis=0)


def thirds(x):
    high = x.astype(BF16).astype(F32)
    middle = (x - high).astype(BF16).astype(F32)
    return high, middle, x - high - middle


def spread(strain, loads):
    blank = [jnp.zeros((GROUP - strain.shape[0] % GROUP, x.shape[1]), F32) for x in (strain, loads)]
    a, b, c = (jnp.concatenate([x, blank[0]], axis=0) for x in thirds(strain))
    d, e, f = (jnp.concatenate([x, blank[1]], axis=0) for x in thirds(loads))
    return lax.dot_general(
        jnp.concatenate([a, a, b, b, a, c], axis=0).astype(BF16),
        jnp.concatenate([d, e, d, e, f, d], axis=0).astype(BF16),
        (((0,), (0,)), ((), ())),
        preferred_element_type=F32,
    )


def strain_of(own, before, after, neighbours_ref):
    points = own.shape[1]
    place = lax.broadcasted_iota(jnp.int32, own.shape, 1)
    left = jnp.where(place == 0, before, pltpu.roll(own, 1, 1))
    right = jnp.where(place == points - 1, after, pltpu.roll(own, points - 1, 1))
    first, second = neighbours_ref[0:1, :], neighbours_ref[1:2, :]
    lower = jnp.where(first == place, left, own)
    upper = jnp.where(second == place + 2, right, own)
    return (upper - lower) / (second - first).astype(F32)


def elastic_kernel(
    per_point,
    blank_ref,
    field_ref,
    neighbours_ref,
    loads_ref,
    stiffness_ref,
    state_ref,
    elastic_ref,
    sum_ref,
    end_ref,
    mode_ref,
    point_ref,
):
    own = stack_rows(field_ref)
    points = own.shape[1]
    modes = state_ref.shape[2]
    tile = TILE * per_point
    strain = strain_of(own, blank_ref[...], blank_ref[...], neighbours_ref)
    loads = stack_rows(loads_ref)
    load = spread(strain, loads)
    loads = jnp.concatenate([loads, jnp.zeros((mode_ref.shape[0] - loads.shape[0], modes), F32)], axis=0)
    stiffness = stiffness_ref[0]
    high, low = halves(jnp.concatenate([load, loads], axis=0))
    shift = dot(high, stiffness) + dot(low, stiffness)
    point_ref[...] = shift[:points, :]
    mode_ref[...] = shift[points:, :]
    tiles = points // TILE
    edge = end_ref.shape[0] // 2
    for t in range(tiles):
        span, at = slice(t * tile, (t + 1) * tile), slice(t * TILE, (t + 1) * TILE)
        acc = dot(state_ref[0, span, :], stiffness)
        acc = acc.reshape(TILE, per_point, modes) + point_ref[at, :][:, None, :]
        elastic_ref[span, :] = acc.reshape(tile, modes).astype(BF16)
        sum_ref[at, :] = jnp.sum(acc, axis=1)
        if t == 0:
            end_ref[:edge, :] = acc.reshape(tile, modes)[:edge, :]
        if t == tiles - 1:
            end_ref[edge:, :] = acc.reshape(tile, modes)[tile - edge :, :]


def plastic_kernel(
    per_point,
    width,
    route_ref,
    core_ref,
    chip_ref,
    field_ref,
    neighbours_ref,
    expand_ref,
    contract_ref,
    flags_ref,
    readout_ref,
    force_ref,
    elastic_ref,
    start_ref,
    end_ref,
    mode_ref,
    out_ref,
    residual_ref,
    next_ref,
    list_ref,
    sum_ref,
    edge_ref,
    hidden_ref,
    bulk_sem,
    edge_sems,
):
    rows, modes = elastic_ref.shape
    points = rows // per_point
    batches = rows // BATCH
    edge = EDGE * per_point
    middle = slice(edge, rows - edge)
    bulk = pltpu.make_async_copy(elastic_ref.at[middle, :], out_ref.at[0, middle, :], bulk_sem)
    bulk.start()
    count = list_alive(route_ref, list_ref, batches)

    odd = lax.axis_index("sub") % 2 == 1
    own, core, chip = stack_rows(field_ref), stack_rows(core_ref), stack_rows(chip_ref)
    before = pltpu.roll(jnp.where(odd, core, chip), 1, 1)
    after = pltpu.roll(jnp.where(odd, chip, core), points - 1, 1)
    blank = jnp.zeros_like(own)
    change = strain_of(own, before, after, neighbours_ref) - strain_of(own, blank, blank, neighbours_ref)
    shifts = [
        jnp.sum(change[:, p : p + 1] * mode_ref[: own.shape[0], :], axis=0, keepdims=True)
        for p in (0, points - 1)
    ]
    ends = [slice(0, edge), slice(rows - edge, rows)]
    fixed = jnp.concatenate(
        [
            end_ref[:per_point, :] + shifts[0],
            end_ref[per_point : 2 * edge - per_point, :],
            end_ref[2 * edge - per_point :, :] + shifts[1],
        ],
        axis=0,
    ).astype(BF16)
    edge_ref[...] = fixed
    sum_ref[...] = start_ref[...]
    sum_ref[0:1, :] = start_ref[0:1, :] + per_point * shifts[0]
    sum_ref[points - 1 : points, :] = start_ref[points - 1 : points, :] + per_point * shifts[1]
    edges = [
        pltpu.make_async_copy(edge_ref.at[i * edge : (i + 1) * edge, :], out_ref.at[0, s, :], edge_sems.at[i])
        for i, s in enumerate(ends)
    ]
    for copy in edges:
        copy.start()

    def chunk(c):
        chosen = [list_ref[jnp.maximum(jnp.minimum(c * width + j, count - 1), 0)] for j in range(width)]
        starts = [pl.multiple_of(b * BATCH, BATCH) for b in chosen]
        parts = []
        for b, s in zip(chosen, starts):
            part = elastic_ref[pl.ds(s, BATCH), :]
            parts.append(jnp.where(b == 0, fixed[:edge, :], part[:edge, :]))
            parts.append(part[edge : BATCH - edge, :])
            parts.append(jnp.where(b == batches - 1, fixed[edge:, :], part[BATCH - edge :, :]))
        taken = jnp.concatenate(parts, axis=0)
        for h in range(0, expand_ref.shape[2], 512):
            hidden_ref[:, h : h + 512] = silu(dot(taken, expand_ref[0, :, h : h + 512])).astype(BF16)
        correction = dot(hidden_ref[...], contract_ref[0])
        p = lax.broadcasted_iota(jnp.int32, (points, BATCH), 0) * per_point
        r = lax.broadcasted_iota(jnp.int32, (points, BATCH), 1)
        owners, changes = [], []
        for j, s in enumerate(starts):
            at = slice(j * BATCH, (j + 1) * BATCH)
            flags = flags_ref[0:1, pl.ds(s, BATCH)].astype(F32)
            column = jnp.broadcast_to(flags, (BATCH, BATCH)).T
            column = jnp.concatenate([column] * (modes // BATCH), axis=1)
            change = column * correction[at, :]
            slot = pl.multiple_of((c * width + j) * BATCH, BATCH)
            next_ref[pl.ds(slot, BATCH), :] = (taken[at, :].astype(F32) + change).astype(BF16)
            row = r + jnp.where(c * width + j < count, s, -rows)
            owners.append(jnp.where((row >= p) & (row < p + per_point), 1.0, 0.0).astype(BF16))
            changes.append(change.astype(BF16))
        sum_ref[...] += dot(jnp.concatenate(owners, axis=1), jnp.concatenate(changes, axis=0))

    pl.loop(0, (count + width - 1) // width)(chunk)

    readout = jnp.broadcast_to(readout_ref[...].astype(F32), (GROUP, modes)).astype(BF16)
    parts = dot_nt(readout, jnp.concatenate(halves(sum_ref[...]), axis=0))[0:1, :]
    mean = (parts[:, :points] + parts[:, points:]) * (1.0 / per_point)
    residual_ref[...] = (force_ref[...] - mean).astype(BF16)
    for copy in [bulk] + edges:
        copy.wait()


def write_kernel(route_ref, next_ref, states_ref, out_ref, list_ref, sem):
    del states_ref
    count = list_alive(route_ref, list_ref, route_ref.shape[2])

    def changed(i):
        source = pl.ds(pl.multiple_of(i * BATCH, BATCH), BATCH)
        target = pl.ds(pl.multiple_of(list_ref[i] * BATCH, BATCH), BATCH)
        return pltpu.make_async_copy(next_ref.at[source, :], out_ref.at[0, target, :], sem)

    @pl.loop(0, count)
    def _(i):
        changed(i).start()

    @pl.loop(0, count)
    def _(i):
        changed(i).wait()


def blank_kernel(blank_ref):
    blank_ref[...] = jnp.zeros_like(blank_ref)


def coarse_kernel(inverse_ref, *refs):
    pairs, out_ref = refs[:-1], refs[-1]
    points = out_ref.shape[1]
    me = lax.axis_index("sub")
    values, columns = [], []
    for k, pair_ref in enumerate(pairs):
        chip = (me // 2) ^ k
        pair = pair_ref[...].astype(F32)
        for c in range(2):
            block = pl.multiple_of((2 * chip + (me + c) % 2) * points, points)
            values.append(jnp.broadcast_to(pair[c : c + 1, :], (GROUP, points)).astype(BF16))
            columns.append(inverse_ref[0, :, pl.ds(block, points)])
    total = dot_nt(jnp.concatenate(values, axis=1), jnp.concatenate(columns, axis=1))
    out_ref[...] = total[0:1, :]


def swap_pairs(n, offset):
    pairs = [(i, i + 1) for i in range(offset, n - 1, 2)]
    return pairs + [(j, i) for i, j in pairs]


def on_device(
    displacement,
    neighbours,
    micro_state,
    strain_loads,
    stiffness,
    expand_weight,
    contract_weight,
    batch_route,
    yield_flags,
    readout,
    external_force,
    coarse_inverse,
):
    n = lax.axis_size("sub")
    points = displacement.shape[2]
    rows, modes = micro_state.shape[1:]
    hidden_size = expand_weight.shape[2]
    per_point = rows // points
    batches = rows // BATCH
    reach = min(16, n // 2, batches)
    width = min(4, reach)
    slots = -(-reach // width) * width
    field = jnp.transpose(displacement, (1, 0, 2))
    loads = jnp.transpose(strain_loads, (1, 0, 2))
    vmem = pl.BlockSpec(memory_space=pltpu.VMEM)
    smem = pl.BlockSpec(memory_space=pltpu.SMEM)
    hbm = pl.BlockSpec(memory_space=pltpu.HBM)
    blank = pl.pallas_call(
        blank_kernel,
        out_shape=jax.ShapeDtypeStruct((displacement.shape[1], points), F32),
        out_specs=vmem,
        compiler_params=pltpu.CompilerParams(vmem_limit_bytes=MIB),
        cost_estimate=pl.CostEstimate(flops=20 * 10**9, bytes_accessed=MIB, transcendentals=0),
    )()
    from_core = lax.ppermute(field, "sub", swap_pairs(n, 0))
    from_chip = lax.ppermute(field, "sub", swap_pairs(n, 1))
    edge = EDGE * per_point
    kinds = -(-displacement.shape[1] // GROUP) * GROUP
    elastic, sums, ends, modes_out = pl.pallas_call(
        functools.partial(elastic_kernel, per_point),
        out_shape=(
            jax.ShapeDtypeStruct((rows, modes), BF16),
            jax.ShapeDtypeStruct((points, modes), F32),
            jax.ShapeDtypeStruct((2 * edge, modes), F32),
            jax.ShapeDtypeStruct((kinds, modes), F32),
        ),
        in_specs=[vmem] * 6,
        out_specs=(vmem,) * 4,
        scratch_shapes=[pltpu.VMEM((points, modes), F32)],
        compiler_params=pltpu.CompilerParams(vmem_limit_bytes=20 * MIB),
        cost_estimate=pl.CostEstimate(
            flops=2 * rows * modes * modes, bytes_accessed=8 * MIB, transcendentals=0
        ),
    )(blank, field, neighbours, loads, stiffness, micro_state)
    states, residual, updated = pl.pallas_call(
        functools.partial(plastic_kernel, per_point, width),
        out_shape=(
            jax.ShapeDtypeStruct((1, rows, modes), BF16),
            jax.ShapeDtypeStruct((1, points), BF16),
            jax.ShapeDtypeStruct((slots * BATCH, modes), BF16),
        ),
        in_specs=[smem] + [vmem] * 13,
        out_specs=(hbm, vmem, vmem),
        scratch_shapes=[
            pltpu.SMEM((batches + 1,), jnp.int32),
            pltpu.VMEM((points, modes), F32),
            pltpu.VMEM((2 * EDGE * per_point, modes), BF16),
            pltpu.VMEM((width * BATCH, hidden_size), BF16),
            pltpu.SemaphoreType.DMA(()),
            pltpu.SemaphoreType.DMA((2,)),
        ],
        compiler_params=pltpu.CompilerParams(vmem_limit_bytes=28 * MIB),
        cost_estimate=pl.CostEstimate(
            flops=4 * width * BATCH * modes * hidden_size, bytes_accessed=8 * MIB, transcendentals=0
        ),
    )(
        batch_route,
        from_core,
        from_chip,
        field,
        neighbours,
        expand_weight,
        contract_weight,
        yield_flags,
        readout,
        external_force,
        elastic,
        sums,
        ends,
        modes_out,
    )
    states_next = pl.pallas_call(
        write_kernel,
        out_shape=jax.ShapeDtypeStruct((1, rows, modes), BF16),
        in_specs=[smem, vmem, hbm],
        out_specs=hbm,
        scratch_shapes=[pltpu.SMEM((batches + 1,), jnp.int32), pltpu.SemaphoreType.DMA(())],
        input_output_aliases={2: 0},
        compiler_params=pltpu.CompilerParams(vmem_limit_bytes=4 * MIB),
        cost_estimate=pl.CostEstimate(flops=0, bytes_accessed=2 * MIB, transcendentals=0),
    )(batch_route, updated, states)
    if n // 2 > NEAR_CHIPS:
        everyone = lax.all_gather(residual, "sub", axis=1, tiled=True)[0]
        return states_next, dot(coarse_inverse[0], everyone)[None]
    other = lax.ppermute(residual, "sub", swap_pairs(n, 0))
    pair = jnp.concatenate([residual, other], axis=0)
    pairs = [pair] + [
        lax.ppermute(pair, "sub", [(i, i ^ (2 * k)) for i in range(n)]) for k in range(1, n // 2)
    ]
    coarse = pl.pallas_call(
        coarse_kernel,
        out_shape=jax.ShapeDtypeStruct((1, points), F32),
        in_specs=[vmem] * (1 + len(pairs)),
        out_specs=vmem,
        compiler_params=pltpu.CompilerParams(vmem_limit_bytes=4 * MIB),
    )(coarse_inverse, *pairs)
    return (states_next, coarse)


def solution(mesh):
    return jax.shard_map(
        on_device,
        mesh=mesh,
        in_specs=(
            P("variant", None, "sub"),
            P(None, "sub"),
            P("variant", "sub", None),
            P("variant", None, None),
            P("variant", None, None),
            P("variant", None, None),
            P("variant", None, None),
            P("variant", None, "sub"),
            P("variant", "sub"),
            P("variant", None),
            P("variant", "sub"),
            P("variant", "sub", None),
        ),
        out_specs=(P("variant", "sub", None), P("variant", "sub")),
        check_vma=False,
    )
```

```python
import functools

import jax
import jax.numpy as jnp
from jax import lax
from jax.experimental import pallas as pl
from jax.experimental.pallas import tpu as pltpu
from jax.sharding import PartitionSpec as P

BATCH = 128
GROUP = 16
TILE = 32
EDGE = 2
NEAR_CHIPS = 4
MIB = 1 << 20
F32 = jnp.float32
BF16 = jnp.bfloat16
NT = (((1,), (1,)), ((), ()))


def dot(a, b):
    return jnp.dot(a, b, preferred_element_type=F32)


def dot_nt(a, b, precision=None):
    return lax.dot_general(a, b, NT, precision=precision, preferred_element_type=F32)


def halves(x):
    high = x.astype(BF16)
    return high, (x - high.astype(F32)).astype(BF16)


def silu(a):
    half = 0.5 * a
    return half + half * jnp.tanh(half)


def list_alive(route_ref, list_ref, batches):
    count = jnp.int32(0)
    for b in range(batches):
        list_ref[count] = jnp.int32(b)
        count = count + (route_ref[0, 0, b] >= 0).astype(jnp.int32)
    return count


def stack_rows(ref):
    return jnp.concatenate([ref[k] for k in range(ref.shape[0])], axis=0)


def thirds(x):
    high = x.astype(BF16).astype(F32)
    middle = (x - high).astype(BF16).astype(F32)
    return high, middle, x - high - middle


def spread(strain, loads):
    blank = [jnp.zeros((GROUP - strain.shape[0] % GROUP, x.shape[1]), F32) for x in (strain, loads)]
    a, b, c = (jnp.concatenate([x, blank[0]], axis=0) for x in thirds(strain))
    d, e, f = (jnp.concatenate([x, blank[1]], axis=0) for x in thirds(loads))
    return lax.dot_general(
        jnp.concatenate([a, a, b, b, a, c], axis=0).astype(BF16),
        jnp.concatenate([d, e, d, e, f, d], axis=0).astype(BF16),
        (((0,), (0,)), ((), ())),
        preferred_element_type=F32,
    )


def strain_of(own, before, after, neighbours_ref):
    points = own.shape[1]
    place = lax.broadcasted_iota(jnp.int32, own.shape, 1)
    left = jnp.where(place == 0, before, pltpu.roll(own, 1, 1))
    right = jnp.where(place == points - 1, after, pltpu.roll(own, points - 1, 1))
    first, second = neighbours_ref[0:1, :], neighbours_ref[1:2, :]
    lower = jnp.where(first == place, left, own)
    upper = jnp.where(second == place + 2, right, own)
    return (upper - lower) / (second - first).astype(F32)


def elastic_kernel(
    per_point,
    blank_ref,
    field_ref,
    neighbours_ref,
    loads_ref,
    stiffness_ref,
    state_ref,
    elastic_ref,
    sum_ref,
    end_ref,
    mode_ref,
    point_ref,
):
    own = stack_rows(field_ref)
    points = own.shape[1]
    modes = state_ref.shape[2]
    tile = TILE * per_point
    strain = strain_of(own, blank_ref[...], blank_ref[...], neighbours_ref)
    loads = stack_rows(loads_ref)
    load = spread(strain, loads)
    loads = jnp.concatenate([loads, jnp.zeros((mode_ref.shape[0] - loads.shape[0], modes), F32)], axis=0)
    stiffness = stiffness_ref[0]
    high, low = halves(jnp.concatenate([load, loads], axis=0))
    shift = dot(high, stiffness) + dot(low, stiffness)
    point_ref[...] = shift[:points, :]
    mode_ref[...] = shift[points:, :]
    tiles = points // TILE
    edge = end_ref.shape[0] // 2
    for t in range(tiles):
        span, at = slice(t * tile, (t + 1) * tile), slice(t * TILE, (t + 1) * TILE)
        acc = dot(state_ref[0, span, :], stiffness)
        acc = acc.reshape(TILE, per_point, modes) + point_ref[at, :][:, None, :]
        elastic_ref[span, :] = acc.reshape(tile, modes).astype(BF16)
        sum_ref[at, :] = jnp.sum(acc, axis=1)
        if t == 0:
            end_ref[:edge, :] = acc.reshape(tile, modes)[:edge, :]
        if t == tiles - 1:
            end_ref[edge:, :] = acc.reshape(tile, modes)[tile - edge :, :]


def plastic_kernel(
    per_point,
    width,
    route_ref,
    core_ref,
    chip_ref,
    field_ref,
    neighbours_ref,
    expand_ref,
    contract_ref,
    flags_ref,
    readout_ref,
    force_ref,
    elastic_ref,
    start_ref,
    end_ref,
    mode_ref,
    out_ref,
    residual_ref,
    next_ref,
    list_ref,
    mean_ref,
    edge_ref,
    hidden_ref,
    bulk_sem,
    edge_sems,
):
    rows, modes = elastic_ref.shape
    points = rows // per_point
    batches = rows // BATCH
    edge = EDGE * per_point
    middle = slice(edge, rows - edge)
    bulk = pltpu.make_async_copy(elastic_ref.at[middle, :], out_ref.at[0, middle, :], bulk_sem)
    bulk.start()
    count = list_alive(route_ref, list_ref, batches)

    odd = lax.axis_index("sub") % 2 == 1
    own, core, chip = stack_rows(field_ref), stack_rows(core_ref), stack_rows(chip_ref)
    before = pltpu.roll(jnp.where(odd, core, chip), 1, 1)
    after = pltpu.roll(jnp.where(odd, chip, core), points - 1, 1)
    blank = jnp.zeros_like(own)
    change = strain_of(own, before, after, neighbours_ref) - strain_of(own, blank, blank, neighbours_ref)
    shifts = [
        jnp.sum(change[:, p : p + 1] * mode_ref[: own.shape[0], :], axis=0, keepdims=True)
        for p in (0, points - 1)
    ]
    ends = [slice(0, edge), slice(rows - edge, rows)]
    fixed = jnp.concatenate(
        [
            end_ref[:per_point, :] + shifts[0],
            end_ref[per_point : 2 * edge - per_point, :],
            end_ref[2 * edge - per_point :, :] + shifts[1],
        ],
        axis=0,
    ).astype(BF16)
    edge_ref[...] = fixed
    readout = jnp.broadcast_to(readout_ref[...].astype(F32), (GROUP, modes))
    first, last = (jnp.sum(shift * readout[0:1, :], axis=1, keepdims=True) for shift in shifts)
    readout = readout.astype(BF16)
    base = dot_nt(readout, jnp.concatenate(halves(start_ref[...]), axis=0))[0:1, :]
    place = lax.broadcasted_iota(jnp.int32, (1, points), 1)
    moved = jnp.where(place == 0, first, 0.0) + jnp.where(place == points - 1, last, 0.0)
    mean_ref[...] = moved + (base[:, :points] + base[:, points:]) * (1.0 / per_point)
    edges = [
        pltpu.make_async_copy(edge_ref.at[i * edge : (i + 1) * edge, :], out_ref.at[0, s, :], edge_sems.at[i])
        for i, s in enumerate(ends)
    ]
    for copy in edges:
        copy.start()

    def chunk(c):
        chosen = [list_ref[jnp.maximum(jnp.minimum(c * width + j, count - 1), 0)] for j in range(width)]
        starts = [pl.multiple_of(b * BATCH, BATCH) for b in chosen]
        parts = []
        for b, s in zip(chosen, starts):
            part = elastic_ref[pl.ds(s, BATCH), :]
            parts.append(jnp.where(b == 0, fixed[:edge, :], part[:edge, :]))
            parts.append(part[edge : BATCH - edge, :])
            parts.append(jnp.where(b == batches - 1, fixed[edge:, :], part[BATCH - edge :, :]))
        taken = jnp.concatenate(parts, axis=0)
        for h in range(0, expand_ref.shape[2], 512):
            hidden_ref[:, h : h + 512] = silu(dot(taken, expand_ref[0, :, h : h + 512])).astype(BF16)
        correction = dot(hidden_ref[...], contract_ref[0])
        p = lax.broadcasted_iota(jnp.int32, (points, BATCH), 0) * per_point
        r = lax.broadcasted_iota(jnp.int32, (points, BATCH), 1)
        owners, changes = [], []
        for j, s in enumerate(starts):
            at = slice(j * BATCH, (j + 1) * BATCH)
            flags = flags_ref[0:1, pl.ds(s, BATCH)].astype(F32)
            column = jnp.broadcast_to(flags, (BATCH, BATCH)).T
            column = jnp.concatenate([column] * (modes // BATCH), axis=1)
            change = column * correction[at, :]
            slot = pl.multiple_of((c * width + j) * BATCH, BATCH)
            next_ref[pl.ds(slot, BATCH), :] = (taken[at, :].astype(F32) + change).astype(BF16)
            row = r + jnp.where(c * width + j < count, s, -rows)
            owners.append(jnp.where((row >= p) & (row < p + per_point), 1.0, 0.0).astype(BF16))
            changes.append(change.astype(BF16))
        high, low = halves(dot_nt(readout, jnp.concatenate(changes, axis=0)))
        share = dot_nt(jnp.concatenate([high, low], axis=0), jnp.concatenate(owners, axis=1))
        mean_ref[...] += (share[0:1, :] + share[GROUP : GROUP + 1, :]) * (1.0 / per_point)

    pl.loop(0, (count + width - 1) // width)(chunk)

    residual_ref[...] = (force_ref[...] - mean_ref[...]).astype(BF16)
    for copy in [bulk] + edges:
        copy.wait()


def write_kernel(route_ref, next_ref, states_ref, out_ref, list_ref, sem):
    del states_ref
    count = list_alive(route_ref, list_ref, route_ref.shape[2])

    def changed(i):
        source = pl.ds(pl.multiple_of(i * BATCH, BATCH), BATCH)
        target = pl.ds(pl.multiple_of(list_ref[i] * BATCH, BATCH), BATCH)
        return pltpu.make_async_copy(next_ref.at[source, :], out_ref.at[0, target, :], sem)

    @pl.loop(0, count)
    def _(i):
        changed(i).start()

    @pl.loop(0, count)
    def _(i):
        changed(i).wait()


def blank_kernel(blank_ref):
    blank_ref[...] = jnp.zeros_like(blank_ref)


def coarse_kernel(inverse_ref, *refs):
    pairs, out_ref = refs[:-1], refs[-1]
    points = out_ref.shape[1]
    me = lax.axis_index("sub")
    values, columns = [], []
    for k, pair_ref in enumerate(pairs):
        chip = (me // 2) ^ k
        pair = pair_ref[...].astype(F32)
        for c in range(2):
            block = pl.multiple_of((2 * chip + (me + c) % 2) * points, points)
            values.append(jnp.broadcast_to(pair[c : c + 1, :], (GROUP, points)).astype(BF16))
            columns.append(inverse_ref[0, :, pl.ds(block, points)])
    total = dot_nt(jnp.concatenate(values, axis=1), jnp.concatenate(columns, axis=1))
    out_ref[...] = total[0:1, :]


def swap_pairs(n, offset):
    pairs = [(i, i + 1) for i in range(offset, n - 1, 2)]
    return pairs + [(j, i) for i, j in pairs]


def on_device(
    displacement,
    neighbours,
    micro_state,
    strain_loads,
    stiffness,
    expand_weight,
    contract_weight,
    batch_route,
    yield_flags,
    readout,
    external_force,
    coarse_inverse,
):
    n = lax.axis_size("sub")
    points = displacement.shape[2]
    rows, modes = micro_state.shape[1:]
    hidden_size = expand_weight.shape[2]
    per_point = rows // points
    batches = rows // BATCH
    reach = min(16, n // 2, batches)
    width = min(4, reach)
    slots = -(-reach // width) * width
    field = jnp.transpose(displacement, (1, 0, 2))
    loads = jnp.transpose(strain_loads, (1, 0, 2))
    vmem = pl.BlockSpec(memory_space=pltpu.VMEM)
    smem = pl.BlockSpec(memory_space=pltpu.SMEM)
    hbm = pl.BlockSpec(memory_space=pltpu.HBM)
    blank = pl.pallas_call(
        blank_kernel,
        out_shape=jax.ShapeDtypeStruct((displacement.shape[1], points), F32),
        out_specs=vmem,
        compiler_params=pltpu.CompilerParams(vmem_limit_bytes=MIB),
        cost_estimate=pl.CostEstimate(flops=20 * 10**9, bytes_accessed=MIB, transcendentals=0),
    )()
    from_core = lax.ppermute(field, "sub", swap_pairs(n, 0))
    from_chip = lax.ppermute(field, "sub", swap_pairs(n, 1))
    edge = EDGE * per_point
    kinds = -(-displacement.shape[1] // GROUP) * GROUP
    elastic, sums, ends, modes_out = pl.pallas_call(
        functools.partial(elastic_kernel, per_point),
        out_shape=(
            jax.ShapeDtypeStruct((rows, modes), BF16),
            jax.ShapeDtypeStruct((points, modes), F32),
            jax.ShapeDtypeStruct((2 * edge, modes), F32),
            jax.ShapeDtypeStruct((kinds, modes), F32),
        ),
        in_specs=[vmem] * 6,
        out_specs=(vmem,) * 4,
        scratch_shapes=[pltpu.VMEM((points, modes), F32)],
        compiler_params=pltpu.CompilerParams(vmem_limit_bytes=20 * MIB),
        cost_estimate=pl.CostEstimate(
            flops=2 * rows * modes * modes, bytes_accessed=8 * MIB, transcendentals=0
        ),
    )(blank, field, neighbours, loads, stiffness, micro_state)
    states, residual, updated = pl.pallas_call(
        functools.partial(plastic_kernel, per_point, width),
        out_shape=(
            jax.ShapeDtypeStruct((1, rows, modes), BF16),
            jax.ShapeDtypeStruct((1, points), BF16),
            jax.ShapeDtypeStruct((slots * BATCH, modes), BF16),
        ),
        in_specs=[smem] + [vmem] * 13,
        out_specs=(hbm, vmem, vmem),
        scratch_shapes=[
            pltpu.SMEM((batches + 1,), jnp.int32),
            pltpu.VMEM((1, points), F32),
            pltpu.VMEM((2 * EDGE * per_point, modes), BF16),
            pltpu.VMEM((width * BATCH, hidden_size), BF16),
            pltpu.SemaphoreType.DMA(()),
            pltpu.SemaphoreType.DMA((2,)),
        ],
        compiler_params=pltpu.CompilerParams(vmem_limit_bytes=28 * MIB),
        cost_estimate=pl.CostEstimate(
            flops=4 * width * BATCH * modes * hidden_size, bytes_accessed=8 * MIB, transcendentals=0
        ),
    )(
        batch_route,
        from_core,
        from_chip,
        field,
        neighbours,
        expand_weight,
        contract_weight,
        yield_flags,
        readout,
        external_force,
        elastic,
        sums,
        ends,
        modes_out,
    )
    states_next = pl.pallas_call(
        write_kernel,
        out_shape=jax.ShapeDtypeStruct((1, rows, modes), BF16),
        in_specs=[smem, vmem, hbm],
        out_specs=hbm,
        scratch_shapes=[pltpu.SMEM((batches + 1,), jnp.int32), pltpu.SemaphoreType.DMA(())],
        input_output_aliases={2: 0},
        compiler_params=pltpu.CompilerParams(vmem_limit_bytes=4 * MIB),
        cost_estimate=pl.CostEstimate(flops=0, bytes_accessed=2 * MIB, transcendentals=0),
    )(batch_route, updated, states)
    if n // 2 > NEAR_CHIPS:
        everyone = lax.all_gather(residual, "sub", axis=1, tiled=True)[0]
        return states_next, dot(coarse_inverse[0], everyone)[None]
    other = lax.ppermute(residual, "sub", swap_pairs(n, 0))
    pair = jnp.concatenate([residual, other], axis=0)
    pairs = [pair] + [
        lax.ppermute(pair, "sub", [(i, i ^ (2 * k)) for i in range(n)]) for k in range(1, n // 2)
    ]
    coarse = pl.pallas_call(
        coarse_kernel,
        out_shape=jax.ShapeDtypeStruct((1, points), F32),
        in_specs=[vmem] * (1 + len(pairs)),
        out_specs=vmem,
        compiler_params=pltpu.CompilerParams(vmem_limit_bytes=4 * MIB),
    )(coarse_inverse, *pairs)
    return (states_next, coarse)


def solution(mesh):
    return jax.shard_map(
        on_device,
        mesh=mesh,
        in_specs=(
            P("variant", None, "sub"),
            P(None, "sub"),
            P("variant", "sub", None),
            P("variant", None, None),
            P("variant", None, None),
            P("variant", None, None),
            P("variant", None, None),
            P("variant", None, "sub"),
            P("variant", "sub"),
            P("variant", None),
            P("variant", "sub"),
            P("variant", "sub", None),
        ),
        out_specs=(P("variant", "sub", None), P("variant", "sub")),
        check_vma=False,
    )
```

```python
import functools

import jax
import jax.numpy as jnp
from jax import lax
from jax.experimental import pallas as pl
from jax.experimental.pallas import tpu as pltpu
from jax.sharding import PartitionSpec as P

BATCH = 128
GROUP = 16
TILE = 32
EDGE = 2
NEAR_CHIPS = 4
MIB = 1 << 20
F32 = jnp.float32
BF16 = jnp.bfloat16
NT = (((1,), (1,)), ((), ()))


def dot(a, b):
    return jnp.dot(a, b, preferred_element_type=F32)


def dot_nt(a, b, precision=None):
    return lax.dot_general(a, b, NT, precision=precision, preferred_element_type=F32)


def halves(x):
    high = x.astype(BF16)
    return high, (x - high.astype(F32)).astype(BF16)


def silu(a):
    half = 0.5 * a
    return half + half * jnp.tanh(half)


def list_alive(route_ref, list_ref, batches):
    count = jnp.int32(0)
    for b in range(batches):
        list_ref[count] = jnp.int32(b)
        count = count + (route_ref[0, 0, b] >= 0).astype(jnp.int32)
    return count


def stack_rows(ref):
    return jnp.concatenate([ref[k] for k in range(ref.shape[0])], axis=0)


def thirds(x):
    high = x.astype(BF16).astype(F32)
    middle = (x - high).astype(BF16).astype(F32)
    return high, middle, x - high - middle


def spread(strain, loads):
    blank = [jnp.zeros((GROUP - strain.shape[0] % GROUP, x.shape[1]), F32) for x in (strain, loads)]
    a, b, c = (jnp.concatenate([x, blank[0]], axis=0) for x in thirds(strain))
    d, e, f = (jnp.concatenate([x, blank[1]], axis=0) for x in thirds(loads))
    return lax.dot_general(
        jnp.concatenate([a, a, b, b, a, c], axis=0).astype(BF16),
        jnp.concatenate([d, e, d, e, f, d], axis=0).astype(BF16),
        (((0,), (0,)), ((), ())),
        preferred_element_type=F32,
    )


def strain_of(own, before, after, neighbours_ref):
    points = own.shape[1]
    place = lax.broadcasted_iota(jnp.int32, own.shape, 1)
    left = jnp.where(place == 0, before, pltpu.roll(own, 1, 1))
    right = jnp.where(place == points - 1, after, pltpu.roll(own, points - 1, 1))
    first, second = neighbours_ref[0:1, :], neighbours_ref[1:2, :]
    lower = jnp.where(first == place, left, own)
    upper = jnp.where(second == place + 2, right, own)
    return (upper - lower) / (second - first).astype(F32)


def elastic_kernel(
    per_point,
    blank_ref,
    field_ref,
    neighbours_ref,
    loads_ref,
    stiffness_ref,
    state_ref,
    elastic_ref,
    sum_ref,
    end_ref,
    mode_ref,
    point_ref,
):
    own = stack_rows(field_ref)
    points = own.shape[1]
    modes = state_ref.shape[2]
    tile = TILE * per_point
    strain = strain_of(own, blank_ref[...], blank_ref[...], neighbours_ref)
    loads = stack_rows(loads_ref)
    load = spread(strain, loads)
    loads = jnp.concatenate([loads, jnp.zeros((mode_ref.shape[0] - loads.shape[0], modes), F32)], axis=0)
    stiffness = stiffness_ref[0]
    high, low = halves(jnp.concatenate([load, loads], axis=0))
    shift = dot(high, stiffness) + dot(low, stiffness)
    point_ref[...] = shift[:points, :]
    mode_ref[...] = shift[points:, :]
    tiles = points // TILE
    edge = end_ref.shape[0] // 2
    for t in range(tiles):
        span, at = slice(t * tile, (t + 1) * tile), slice(t * TILE, (t + 1) * TILE)
        acc = dot(state_ref[0, span, :], stiffness)
        acc = acc.reshape(TILE, per_point, modes) + point_ref[at, :][:, None, :]
        elastic_ref[span, :] = acc.reshape(tile, modes).astype(BF16)
        sum_ref[at, :] = jnp.sum(acc, axis=1)
        if t == 0:
            end_ref[:edge, :] = acc.reshape(tile, modes)[:edge, :]
        if t == tiles - 1:
            end_ref[edge:, :] = acc.reshape(tile, modes)[tile - edge :, :]


def plastic_kernel(
    per_point,
    width,
    route_ref,
    chip_ref,
    core_ref,
    field_ref,
    neighbours_ref,
    expand_ref,
    contract_ref,
    flags_ref,
    readout_ref,
    force_ref,
    elastic_ref,
    start_ref,
    end_ref,
    mode_ref,
    out_ref,
    residual_ref,
    next_ref,
    list_ref,
    mean_ref,
    edge_ref,
    hidden_ref,
    bulk_sem,
    edge_sems,
):
    rows, modes = elastic_ref.shape
    points = rows // per_point
    batches = rows // BATCH
    edge = EDGE * per_point
    middle = slice(edge, rows - edge)
    bulk = pltpu.make_async_copy(elastic_ref.at[middle, :], out_ref.at[0, middle, :], bulk_sem)
    bulk.start()
    count = list_alive(route_ref, list_ref, batches)

    odd = lax.axis_index("sub") % 2 == 1
    own, core, chip = stack_rows(field_ref), stack_rows(core_ref), stack_rows(chip_ref)
    before = pltpu.roll(jnp.where(odd, core, chip), 1, 1)
    after = pltpu.roll(jnp.where(odd, chip, core), points - 1, 1)
    blank = jnp.zeros_like(own)
    change = strain_of(own, before, after, neighbours_ref) - strain_of(own, blank, blank, neighbours_ref)
    shifts = [
        jnp.sum(change[:, p : p + 1] * mode_ref[: own.shape[0], :], axis=0, keepdims=True)
        for p in (0, points - 1)
    ]
    ends = [slice(0, edge), slice(rows - edge, rows)]
    fixed = jnp.concatenate(
        [
            end_ref[:per_point, :] + shifts[0],
            end_ref[per_point : 2 * edge - per_point, :],
            end_ref[2 * edge - per_point :, :] + shifts[1],
        ],
        axis=0,
    ).astype(BF16)
    edge_ref[...] = fixed
    readout = jnp.broadcast_to(readout_ref[...].astype(F32), (GROUP, modes))
    first, last = (jnp.sum(shift * readout[0:1, :], axis=1, keepdims=True) for shift in shifts)
    readout = readout.astype(BF16)
    base = dot_nt(readout, jnp.concatenate(halves(start_ref[...]), axis=0))[0:1, :]
    place = lax.broadcasted_iota(jnp.int32, (1, points), 1)
    moved = jnp.where(place == 0, first, 0.0) + jnp.where(place == points - 1, last, 0.0)
    mean_ref[...] = moved + (base[:, :points] + base[:, points:]) * (1.0 / per_point)
    edges = [
        pltpu.make_async_copy(edge_ref.at[i * edge : (i + 1) * edge, :], out_ref.at[0, s, :], edge_sems.at[i])
        for i, s in enumerate(ends)
    ]
    for copy in edges:
        copy.start()

    def chunk(c):
        chosen = [list_ref[jnp.maximum(jnp.minimum(c * width + j, count - 1), 0)] for j in range(width)]
        starts = [pl.multiple_of(b * BATCH, BATCH) for b in chosen]
        parts = []
        for b, s in zip(chosen, starts):
            part = elastic_ref[pl.ds(s, BATCH), :]
            parts.append(jnp.where(b == 0, fixed[:edge, :], part[:edge, :]))
            parts.append(part[edge : BATCH - edge, :])
            parts.append(jnp.where(b == batches - 1, fixed[edge:, :], part[BATCH - edge :, :]))
        taken = jnp.concatenate(parts, axis=0)
        for h in range(0, expand_ref.shape[2], 512):
            hidden_ref[:, h : h + 512] = silu(dot(taken, expand_ref[0, :, h : h + 512])).astype(BF16)
        correction = dot(hidden_ref[...], contract_ref[0])
        p = lax.broadcasted_iota(jnp.int32, (points, BATCH), 0) * per_point
        r = lax.broadcasted_iota(jnp.int32, (points, BATCH), 1)
        owners, changes = [], []
        for j, s in enumerate(starts):
            at = slice(j * BATCH, (j + 1) * BATCH)
            flags = flags_ref[0:1, pl.ds(s, BATCH)].astype(F32)
            column = jnp.broadcast_to(flags, (BATCH, BATCH)).T
            column = jnp.concatenate([column] * (modes // BATCH), axis=1)
            change = column * correction[at, :]
            slot = pl.multiple_of((c * width + j) * BATCH, BATCH)
            next_ref[pl.ds(slot, BATCH), :] = (taken[at, :].astype(F32) + change).astype(BF16)
            row = r + jnp.where(c * width + j < count, s, -rows)
            owners.append(jnp.where((row >= p) & (row < p + per_point), 1.0, 0.0).astype(BF16))
            changes.append(change.astype(BF16))
        high, low = halves(dot_nt(readout, jnp.concatenate(changes, axis=0)))
        share = dot_nt(jnp.concatenate([high, low], axis=0), jnp.concatenate(owners, axis=1))
        mean_ref[...] += (share[0:1, :] + share[GROUP : GROUP + 1, :]) * (1.0 / per_point)

    pl.loop(0, (count + width - 1) // width)(chunk)

    residual_ref[...] = (force_ref[...] - mean_ref[...]).astype(BF16)
    for copy in [bulk] + edges:
        copy.wait()


def write_kernel(route_ref, next_ref, states_ref, out_ref, list_ref, sem):
    del states_ref
    count = list_alive(route_ref, list_ref, route_ref.shape[2])

    def changed(i):
        source = pl.ds(pl.multiple_of(i * BATCH, BATCH), BATCH)
        target = pl.ds(pl.multiple_of(list_ref[i] * BATCH, BATCH), BATCH)
        return pltpu.make_async_copy(next_ref.at[source, :], out_ref.at[0, target, :], sem)

    @pl.loop(0, count)
    def _(i):
        changed(i).start()

    @pl.loop(0, count)
    def _(i):
        changed(i).wait()


def blank_kernel(blank_ref):
    blank_ref[...] = jnp.zeros_like(blank_ref)


def coarse_kernel(inverse_ref, *refs):
    pairs, out_ref = refs[:-1], refs[-1]
    points = out_ref.shape[1]
    me = lax.axis_index("sub")
    values, columns = [], []
    for k, pair_ref in enumerate(pairs):
        chip = (me // 2) ^ k
        pair = pair_ref[...].astype(F32)
        for c in range(2):
            block = pl.multiple_of((2 * chip + (me + c) % 2) * points, points)
            values.append(jnp.broadcast_to(pair[c : c + 1, :], (GROUP, points)).astype(BF16))
            columns.append(inverse_ref[0, :, pl.ds(block, points)])
    total = dot_nt(jnp.concatenate(values, axis=1), jnp.concatenate(columns, axis=1))
    out_ref[...] = total[0:1, :]


def swap_pairs(n, offset):
    pairs = [(i, i + 1) for i in range(offset, n - 1, 2)]
    return pairs + [(j, i) for i, j in pairs]


def on_device(
    displacement,
    neighbours,
    micro_state,
    strain_loads,
    stiffness,
    expand_weight,
    contract_weight,
    batch_route,
    yield_flags,
    readout,
    external_force,
    coarse_inverse,
):
    n = lax.axis_size("sub")
    points = displacement.shape[2]
    rows, modes = micro_state.shape[1:]
    hidden_size = expand_weight.shape[2]
    per_point = rows // points
    batches = rows // BATCH
    reach = min(16, n // 2, batches)
    width = min(4, reach)
    slots = -(-reach // width) * width
    field = jnp.transpose(displacement, (1, 0, 2))
    loads = jnp.transpose(strain_loads, (1, 0, 2))
    vmem = pl.BlockSpec(memory_space=pltpu.VMEM)
    smem = pl.BlockSpec(memory_space=pltpu.SMEM)
    hbm = pl.BlockSpec(memory_space=pltpu.HBM)
    blank = pl.pallas_call(
        blank_kernel,
        out_shape=jax.ShapeDtypeStruct((displacement.shape[1], points), F32),
        out_specs=vmem,
        compiler_params=pltpu.CompilerParams(vmem_limit_bytes=MIB),
        cost_estimate=pl.CostEstimate(flops=20 * 10**9, bytes_accessed=MIB, transcendentals=0),
    )()
    from_core = lax.ppermute(field, "sub", swap_pairs(n, 0))
    from_chip = lax.ppermute(field, "sub", swap_pairs(n, 1))
    edge = EDGE * per_point
    kinds = -(-displacement.shape[1] // GROUP) * GROUP
    elastic, sums, ends, modes_out = pl.pallas_call(
        functools.partial(elastic_kernel, per_point),
        out_shape=(
            jax.ShapeDtypeStruct((rows, modes), BF16),
            jax.ShapeDtypeStruct((points, modes), F32),
            jax.ShapeDtypeStruct((2 * edge, modes), F32),
            jax.ShapeDtypeStruct((kinds, modes), F32),
        ),
        in_specs=[vmem] * 6,
        out_specs=(vmem,) * 4,
        scratch_shapes=[pltpu.VMEM((points, modes), F32)],
        compiler_params=pltpu.CompilerParams(vmem_limit_bytes=20 * MIB),
        cost_estimate=pl.CostEstimate(
            flops=2 * rows * modes * modes, bytes_accessed=8 * MIB, transcendentals=0
        ),
    )(blank, field, neighbours, loads, stiffness, micro_state)
    states, residual, updated = pl.pallas_call(
        functools.partial(plastic_kernel, per_point, width),
        out_shape=(
            jax.ShapeDtypeStruct((1, rows, modes), BF16),
            jax.ShapeDtypeStruct((1, points), BF16),
            jax.ShapeDtypeStruct((slots * BATCH, modes), BF16),
        ),
        in_specs=[smem] + [vmem] * 13,
        out_specs=(hbm, vmem, vmem),
        scratch_shapes=[
            pltpu.SMEM((batches + 1,), jnp.int32),
            pltpu.VMEM((1, points), F32),
            pltpu.VMEM((2 * EDGE * per_point, modes), BF16),
            pltpu.VMEM((width * BATCH, hidden_size), BF16),
            pltpu.SemaphoreType.DMA(()),
            pltpu.SemaphoreType.DMA((2,)),
        ],
        compiler_params=pltpu.CompilerParams(vmem_limit_bytes=28 * MIB),
        cost_estimate=pl.CostEstimate(
            flops=4 * width * BATCH * modes * hidden_size, bytes_accessed=8 * MIB, transcendentals=0
        ),
    )(
        batch_route,
        from_chip,
        from_core,
        field,
        neighbours,
        expand_weight,
        contract_weight,
        yield_flags,
        readout,
        external_force,
        elastic,
        sums,
        ends,
        modes_out,
    )
    states_next = pl.pallas_call(
        write_kernel,
        out_shape=jax.ShapeDtypeStruct((1, rows, modes), BF16),
        in_specs=[smem, vmem, hbm],
        out_specs=hbm,
        scratch_shapes=[pltpu.SMEM((batches + 1,), jnp.int32), pltpu.SemaphoreType.DMA(())],
        input_output_aliases={2: 0},
        compiler_params=pltpu.CompilerParams(vmem_limit_bytes=4 * MIB),
        cost_estimate=pl.CostEstimate(flops=0, bytes_accessed=2 * MIB, transcendentals=0),
    )(batch_route, updated, states)
    if n // 2 > NEAR_CHIPS:
        everyone = lax.all_gather(residual, "sub", axis=1, tiled=True)[0]
        return states_next, dot(coarse_inverse[0], everyone)[None]
    other = lax.ppermute(residual, "sub", swap_pairs(n, 0))
    pair = jnp.concatenate([residual, other], axis=0)
    pairs = [pair] + [
        lax.ppermute(pair, "sub", [(i, i ^ (2 * k)) for i in range(n)]) for k in range(1, n // 2)
    ]
    coarse = pl.pallas_call(
        coarse_kernel,
        out_shape=jax.ShapeDtypeStruct((1, points), F32),
        in_specs=[vmem] * (1 + len(pairs)),
        out_specs=vmem,
        compiler_params=pltpu.CompilerParams(vmem_limit_bytes=4 * MIB),
    )(coarse_inverse, *pairs)
    return (states_next, coarse)


def solution(mesh):
    return jax.shard_map(
        on_device,
        mesh=mesh,
        in_specs=(
            P("variant", None, "sub"),
            P(None, "sub"),
            P("variant", "sub", None),
            P("variant", None, None),
            P("variant", None, None),
            P("variant", None, None),
            P("variant", None, None),
            P("variant", None, "sub"),
            P("variant", "sub"),
            P("variant", None),
            P("variant", "sub"),
            P("variant", "sub", None),
        ),
        out_specs=(P("variant", "sub", None), P("variant", "sub")),
        check_vma=False,
    )
```
